512 devices in a mesh: dp: 32 (over x, y, core), expert: 16 (over z).
Axes of the slice: x: 4, y: 4, z: 16, core: 2. Of those that a mesh axis runs over, the one named last changes fastest.
Arguments:
- tokens: bfloat16 [65536, 2048], P(('dp', 'expert')), may hold values from -24 to 24
- cotangent: bfloat16 [65536, 2048], P(('dp', 'expert')), may hold values from -6 to 6
- expert_ids: int32 [65536, 8], P(('dp', 'expert')), may hold values from 0 to 127, as said below
- drop_mask: int32 [65536, 8], P(('dp', 'expert')), may hold values 0 or 1
- gate_table: float32 [65536, 8], P(('dp', 'expert')), may hold values from 0.1 to 1
- gate_weight: bfloat16 [2048, 3072], P('dp', 'expert'), may hold values from -0.125 to 0.125
- up_weight: bfloat16 [2048, 3072], P('dp', 'expert'), may hold values from -0.125 to 0.125
- down_weight: bfloat16 [3072, 2048], P('expert', 'dp'), may hold values from -0.21875 to 0.21875
Outputs:
- grad_tokens: bfloat16 [65536, 2048], P(('dp', 'expert'))
- grad_gate: float32 [2048, 3072], P('dp', 'expert')
- grad_up: float32 [2048, 3072], P('dp', 'expert')
- grad_down: float32 [3072, 2048], P('expert', 'dp')
The draws below stay inside these ranges and needn't reach their ends.
Inputs may be any that keep to these rules, and one draw needn't show every extreme that they name: `expert_ids`: each row names 8 different experts.
All inputs are finite; a program needn't handle non-finite values. No bound on the sum of `drop_mask` on one device may be relied on, other than what follows from the above.
Results may differ from the reference program's by a relative error of at most 0.018.
Values may be sent and summed in bfloat16 or wider, within the bound.
A program may use at most 64 MiB of HBM per device.

```python
import math
import jax
import jax.numpy as jnp
from jax import lax

D = 2048
FF = 768
EXPERTS = 128
TOP = 8
SPLIT = 4
TOK_DEV = 128
CAP = 16
FLIGHT = 4
TOKENS = 65536
GROUPS = 32


def draw_expert_ids(key, part):
    key = jax.random.fold_in(key, 11)
    base_key, roll_key = jax.random.split(key)
    base_score = jax.random.randint(base_key, (TOKENS, EXPERTS), 0, 1 << 20)
    roll = jax.random.randint(roll_key, (TOKENS, EXPERTS), 0, 1000)
    column = jnp.arange(EXPERTS, dtype=jnp.int32)
    chance = jnp.where(column < FLIGHT, 250 // (1 + column), 0)
    forced = (roll < chance[None, :]).astype(jnp.int32)
    score = (base_score + forced * (1 << 21)) * EXPERTS + column[None, :]
    picked_values, picked = lax.top_k(score, TOP)
    return picked.astype(jnp.int32)


def set_ends(values, stream_key, low, top_value):
    longest = values.shape.index(max(values.shape))
    spots = []
    for shift in (0, 1):
        where = [jax.random.randint(jax.random.fold_in(stream_key, axis), (), 0, length) for axis, length in enumerate(values.shape)]
        where[longest] = (where[longest] + shift) % values.shape[longest]
        spots.append(tuple(where))
    return values.at[spots[0]].set(low).at[spots[1]].set(top_value)


def with_spikes(values, own_key, source, target, blocks, factor):
    owner, partner = [(jnp.arange(values.shape[dim]) // (values.shape[dim] // blocks)).reshape([-1 if axis == dim else 1 for axis in range(values.ndim)]) for dim in (source, target)]
    chosen = jax.random.permutation(own_key, blocks)[partner]
    strong = (owner == chosen) | (owner == (partner + blocks // 2) % blocks)
    return jnp.where(strong, factor * values, values)


def shard_levels(key, shape, cuts, least, largest):
    level = 1.0
    for position, blocks in cuts:
        heights = jax.random.uniform(jax.random.fold_in(jax.random.fold_in(key, 6), position), (blocks,), jnp.float32, least / len(cuts), largest / len(cuts))
        level = level * jnp.repeat(jnp.exp(heights), shape[position] // blocks).reshape((-1,) + (1,) * (len(shape) - 1 - position))
    return level


def scatter_about(own_key, shape, spread, most, shards=(), kind=jnp.bfloat16):
    entries = spread * jax.random.normal(own_key, shape, jnp.float32)
    if shards:
        entries = entries * shard_levels(own_key, shape, shards, -0.22, 0.18)
    return jnp.clip(entries, -most, most).astype(kind)


def heavy_noise(rng, shape, deviation, most, cuts, heavy, kind=jnp.bfloat16):
    result = deviation * jax.random.normal(rng, shape, jnp.float32)
    if cuts:
        result = result * shard_levels(rng, shape, cuts, -0.22, 0.18)
    return jnp.clip(with_spikes(result, jax.random.fold_in(rng, 3), *heavy), -most, most).astype(kind)


def setup_inputs(seed: int = 0) -> dict:
    keys = jax.random.split(jax.random.key(seed), 9)
    return {
        "tokens": heavy_noise(keys[0], (TOKENS, D), 1.0, 24.0, ((0, 512),), (0, 1, 512, 6.0)),
        "cotangent": scatter_about(keys[1], (TOKENS, D), 1.0, 6.0, ((0, 512),)),
        "expert_ids": draw_expert_ids(jax.random.fold_in(keys[8], 71), 0),
        "drop_mask": set_ends((jax.random.randint(keys[3], (TOKENS, TOP), 0, 8) < 7).astype(jnp.int32), jax.random.fold_in(keys[3], 1), 0, 1),
        "gate_table": jnp.clip(jnp.exp(math.log(1.0) - 2.3025851 * jax.random.uniform(keys[4], (TOKENS, TOP), jnp.float32) ** shard_levels(keys[4], (TOKENS, TOP), ((0, 512),), -0.2, 0.2)), 0.1, 1.0),
        "gate_weight": scatter_about(keys[5], (D, FLIGHT * FF), D ** -0.5, 0.125, ((0, 32), (1, 16))),
        "up_weight": scatter_about(keys[6], (D, FLIGHT * FF), D ** -0.5, 0.125, ((0, 32), (1, 16))),
        "down_weight": scatter_about(keys[7], (FLIGHT * FF, D), FF ** -0.5, 0.21875, ((0, 16), (1, 32))),
    }


def silu_parts(pre_gate):
    sigmoid_value = jax.nn.sigmoid(pre_gate)
    return pre_gate * sigmoid_value, sigmoid_value * (1.0 + pre_gate * (1.0 - sigmoid_value))


def slot_table(expert_ids, drop_mask, block_rows, in_flight):
    window = jnp.arange(in_flight, dtype=jnp.int32)
    hit_table = ((expert_ids[:, :, None] == window[None, None, :]) & (drop_mask[:, :, None] == 1)).astype(jnp.int32)
    per_token = jnp.sum(hit_table, axis=1)
    blocked = per_token.reshape(-1, block_rows, in_flight)
    earlier = (jnp.cumsum(blocked, axis=1) - blocked).reshape(-1, in_flight)
    slot_rank = jnp.sum(hit_table * earlier[:, None, :], axis=2)
    is_live = (jnp.sum(hit_table, axis=2) > 0) & (slot_rank < CAP)
    return jnp.where(is_live, expert_ids * CAP + slot_rank, in_flight * CAP).astype(jnp.int32)


def group_sum(left_rows, right_rows):
    left_groups = left_rows.reshape(GROUPS, -1, left_rows.shape[1]).astype(jnp.float32)
    right_groups = right_rows.reshape(GROUPS, -1, right_rows.shape[1]).astype(jnp.float32)
    partial_sums = jnp.einsum("gri,grf->gif", left_groups, right_groups)
    rounded = lax.optimization_barrier(partial_sums.astype(jnp.bfloat16))
    return jnp.sum(rounded.astype(jnp.float32), axis=0)


def reference(tokens, cotangent, expert_ids, drop_mask, gate_table, gate_weight, up_weight, down_weight):
    blocks = TOKENS // TOK_DEV
    per_block = FLIGHT * CAP
    buffer_rows = blocks * per_block
    part_width = FF // SPLIT
    local = slot_table(expert_ids, drop_mask, TOK_DEV, FLIGHT)
    block_of = (jnp.arange(TOKENS, dtype=jnp.int32) // TOK_DEV)[:, None]
    token_of = jnp.broadcast_to(jnp.arange(TOKENS, dtype=jnp.int32)[:, None], (TOKENS, TOP))
    global_slot = jnp.where(local < per_block, block_of * per_block + local, buffer_rows).astype(jnp.int32).reshape(-1)
    slot_token = jnp.zeros((buffer_rows,), jnp.int32).at[global_slot].set(token_of.reshape(-1), mode="drop")
    slot_gate = jnp.zeros((buffer_rows,), jnp.float32).at[global_slot].set(gate_table.reshape(-1).astype(jnp.float32), mode="drop")
    filled = jnp.zeros((buffer_rows,), jnp.float32).at[global_slot].set(1.0, mode="drop")
    expert_in = jnp.where(filled[:, None] > 0, tokens[slot_token], jnp.zeros((), tokens.dtype))
    expert_grad = (slot_gate[:, None] * cotangent[slot_token].astype(jnp.float32)).astype(jnp.bfloat16)
    expert_in = expert_in.reshape(blocks, FLIGHT, CAP, D)
    expert_grad = expert_grad.reshape(blocks, FLIGHT, CAP, D)
    slot_grads = []
    gate_grads = []
    up_grads = []
    down_grads = []
    for expert in range(FLIGHT):
        rows_in = expert_in[:, expert].reshape(-1, D)
        rows_grad = expert_grad[:, expert].reshape(-1, D)
        gate_cols = gate_weight[:, expert * FF:(expert + 1) * FF]
        up_cols = up_weight[:, expert * FF:(expert + 1) * FF]
        down_rows = down_weight[expert * FF:(expert + 1) * FF, :]
        pre_gate = jnp.dot(rows_in, gate_cols, preferred_element_type=jnp.float32)
        pre_up = jnp.dot(rows_in, up_cols, preferred_element_type=jnp.float32)
        silu_value, silu_slope = silu_parts(pre_gate)
        activated = (silu_value * pre_up).astype(jnp.bfloat16)
        grad_act = jnp.dot(rows_grad, down_rows.T, preferred_element_type=jnp.float32)
        grad_gate_pre = (grad_act * pre_up * silu_slope).astype(jnp.bfloat16)
        grad_up_pre = (grad_act * silu_value).astype(jnp.bfloat16)
        slot_grad = jnp.zeros((rows_in.shape[0], D), jnp.float32)
        for part in range(SPLIT):
            low = part * part_width
            high = low + part_width
            slot_part = jnp.dot(grad_gate_pre[:, low:high], gate_cols[:, low:high].T, preferred_element_type=jnp.float32) + jnp.dot(grad_up_pre[:, low:high], up_cols[:, low:high].T, preferred_element_type=jnp.float32)
            slot_grad = slot_grad + slot_part.astype(jnp.bfloat16).astype(jnp.float32)
        slot_grads.append(slot_grad.reshape(blocks, CAP, D))
        gate_grads.append(group_sum(rows_in, grad_gate_pre))
        up_grads.append(group_sum(rows_in, grad_up_pre))
        down_grads.append(group_sum(activated, rows_grad))
    all_slots = jnp.stack(slot_grads, axis=1).reshape(buffer_rows, D)
    grad_tokens = jnp.zeros((TOKENS, D), jnp.float32).at[slot_token].add(all_slots * filled[:, None])
    return (grad_tokens.astype(jnp.bfloat16), jnp.concatenate(gate_grads, axis=1), jnp.concatenate(up_grads, axis=1), jnp.concatenate(down_grads, axis=0))
```

```python
import functools

import jax
import jax.numpy as jnp
from jax import lax
from jax.experimental import pallas as pl
from jax.experimental.pallas import tpu as pltpu
from jax.sharding import PartitionSpec as P

MESH = pl.DeviceIdType.MESH
RING = 16
SPLIT = 4
CAP = 16
FAR = SPLIT + 2
REACH = FAR + SPLIT - 1
LAST = (((1,), (1,)), ((), ()))
FIRST = (((0,), (0,)), ((), ()))


def copy_to(src, dst, send_sem, recv_sem, device):
    return pltpu.make_async_remote_copy(
        src_ref=src,
        dst_ref=dst,
        send_sem=send_sem,
        recv_sem=recv_sem,
        device_id=device,
        device_id_type=MESH,
    )


def kernel(
    tokens,
    cotangent,
    ids,
    mask,
    gates,
    gate_w,
    up_w,
    down_w,
    grad_tokens,
    grad_gate,
    grad_up,
    grad_down,
    place,
    out_in,
    out_grad,
    rows_in,
    rows_grad,
    weights,
    pre,
    act,
    pair,
    active,
    parts,
    from_right,
    from_left,
    finals,
    grads,
    sibling_grads,
    grads_in,
    direct_send,
    pass_right,
    pass_left,
    rows_recv,
    weight_send,
    weight_recv,
    back_left,
    back_right,
    right_recv,
    left_recv,
    final_recv,
    sibling_send,
    sibling_recv,
    grad_send,
    grad_recv,
):
    width = tokens.shape[1]
    hidden = gate_w.shape[1]
    depth = gate_w.shape[0]
    n_dp = weights.shape[0]
    half = n_dp // 2
    n_tok = tokens.shape[0]
    n_rows = RING * CAP
    step = min(256, width // 2)
    blocks = step // depth
    lanes = weights.shape[2]

    dp = lax.axis_index("dp")
    z = lax.axis_index("expert")
    group = z // SPLIT
    member = lax.rem(z, SPLIT)
    core = lax.rem(dp, 2)
    chip = dp // 2
    sibling = dp + 1 - 2 * core

    def plane(offset):
        return (dp, lax.rem(z + offset + RING, RING))

    barrier = pltpu.get_barrier_semaphore()

    def greet_ring(i, carry):
        pl.semaphore_signal(barrier, inc=1, device_id=plane(i), device_id_type=MESH)
        return carry

    def greet_plane(i, carry):
        pl.semaphore_signal(
            barrier, inc=1, device_id=(lax.rem(dp + i, n_dp), z), device_id_type=MESH
        )
        return carry

    lax.fori_loop(1, RING, greet_ring, 0)
    lax.fori_loop(1, n_dp, greet_plane, 0)

    live = mask[...] == 1
    hits, gate_rows = [], []
    for j in range(SPLIT):
        hit = jnp.where((ids[...] == j) & live, 1.0, 0.0)
        hits.append(jnp.sum(hit, axis=0, keepdims=True))
        gate_rows.append(jnp.sum(hit * gates[...], axis=0, keepdims=True))
    hit_rows = jnp.concatenate(hits + [jnp.zeros((CAP - SPLIT, n_tok), jnp.float32)], axis=0)
    earlier = (
        lax.broadcasted_iota(jnp.int32, (n_tok, n_tok), 0)
        < lax.broadcasted_iota(jnp.int32, (n_tok, n_tok), 1)
    )
    rank = jnp.dot(
        hit_rows.astype(jnp.bfloat16),
        jnp.where(earlier, 1.0, 0.0).astype(jnp.bfloat16),
        preferred_element_type=jnp.float32,
    )
    slot = lax.broadcasted_iota(jnp.int32, (CAP, n_tok), 0).astype(jnp.float32)
    slot_gates = []
    for j in range(SPLIT):
        held = jnp.where(
            (jnp.broadcast_to(rank[j : j + 1], (CAP, n_tok)) == slot)
            & (jnp.broadcast_to(hits[j], (CAP, n_tok)) > 0.5),
            1.0,
            0.0,
        )
        place[j] = held.astype(jnp.bfloat16)
        slot_gates.append(jnp.sum(held * gate_rows[j], axis=1, keepdims=True))
    slot_gate = jnp.concatenate(slot_gates, axis=0)
    chosen = place[...].reshape(SPLIT * CAP, n_tok)

    def fill(c, carry):
        cols = pl.ds(pl.multiple_of(c * step, step), step)
        picked = jnp.dot(chosen, tokens[:, cols], preferred_element_type=jnp.float32)
        out_in[:, :, cols] = picked.astype(jnp.bfloat16).reshape(SPLIT, CAP, step)
        picked = jnp.dot(chosen, cotangent[:, cols], preferred_element_type=jnp.float32)
        out_grad[:, :, cols] = (
            (slot_gate * picked).astype(jnp.bfloat16).reshape(SPLIT, CAP, step)
        )
        return carry

    lax.fori_loop(0, width // step, fill, 0)

    packed = jnp.concatenate(
        [
            gate_w[...].astype(jnp.float32),
            up_w[...].astype(jnp.float32),
            down_w[...].astype(jnp.float32),
            jnp.zeros((depth, lanes - 3 * hidden), jnp.float32),
        ],
        axis=1,
    )
    weights[dp] = packed.astype(jnp.bfloat16)

    pl.semaphore_wait(barrier, RING - 1 + n_dp - 1)

    upper = member // 2
    both = ((out_in, rows_in), (out_grad, rows_grad))

    def direct(index, offset, slot_there, expert):
        for h, (source, rows) in enumerate(both):
            yield copy_to(
                source.at[expert],
                rows.at[slot_there],
                direct_send.at[index, h],
                rows_recv.at[slot_there, h],
                plane(offset),
            )

    far = list(
        direct(
            0,
            upper * (8 - member) - (1 - upper) * (member + 5),
            upper * (8 + member) + (1 - upper) * (member + 5),
            lax.rem(group + 2, SPLIT),
        )
    )
    near = list(direct(1, 4 - member, 12 + member, lax.rem(group + 1, SPLIT)))
    near += list(direct(2, -(member + 1), member + 1, lax.rem(group + 3, SPLIT)))
    own_right = list(direct(3, 1, RING - 1, group))
    own_left = list(direct(4, -1, 1, group))

    @pl.when(member < SPLIT - 1)
    def _():
        for copy in own_right:
            copy.start()

    @pl.when(member > 0)
    def _():
        for copy in own_left:
            copy.start()

    for copy in near + far:
        copy.start()

    def weight_copy(i):
        return copy_to(
            weights.at[dp],
            weights.at[dp],
            weight_send.at[i],
            weight_recv.at[dp],
            (lax.rem(dp + i, n_dp), z),
        )

    def send_weights(i, carry):
        weight_copy(i).start()
        return carry

    lax.fori_loop(1, n_dp, send_weights, 0)

    rows_in[0] = out_in[group]
    rows_grad[0] = out_grad[group]

    def right_pass(k, h, rows):
        return copy_to(
            rows.at[RING - k],
            rows.at[RING - k - 1],
            pass_right.at[k, h],
            rows_recv.at[RING - k - 1, h],
            plane(1),
        )

    def left_pass(k, h, rows):
        return copy_to(
            rows.at[k],
            rows.at[k + 1],
            pass_left.at[k, h],
            rows_recv.at[k + 1, h],
            plane(-1),
        )

    def arrived(slot_here, h, rows):
        copy_to(
            rows.at[slot_here],
            rows.at[slot_here],
            direct_send.at[0, h],
            rows_recv.at[slot_here, h],
            plane(1),
        ).wait_recv()

    def pass_rows(k, carry):
        @pl.when(k <= member + FAR)
        def _():
            for h, (_, rows) in enumerate(both):
                arrived(RING - k, h, rows)

                @pl.when(member < SPLIT - 1)
                def _():
                    right_pass(k, h, rows).start()

        @pl.when(k <= REACH - member)
        def _():
            for h, (_, rows) in enumerate(both):
                arrived(k, h, rows)

                @pl.when(member > 0)
                def _():
                    left_pass(k, h, rows).start()

        return carry

    lax.fori_loop(1, REACH + 1, pass_rows, 0)

    def weights_arrived(i, carry):
        source = lax.rem(dp + i, n_dp)
        copy_to(
            weights.at[source],
            weights.at[source],
            weight_send.at[i],
            weight_recv.at[source],
            (sibling, z),
        ).wait_recv()
        return carry

    lax.fori_loop(1, n_dp, weights_arrived, 0)

    pre[...] = jnp.zeros_like(pre)
    act[...] = jnp.zeros_like(act)

    def project(c, carry):
        cols = pl.ds(pl.multiple_of(c * step, step), step)
        block = weights[pl.ds(c * blocks, blocks)].reshape(step, lanes)
        left = rows_in[:, :, cols].reshape(n_rows, step)
        pre[...] += jnp.dot(left, block[:, : 2 * hidden], preferred_element_type=jnp.float32)
        left = rows_grad[:, :, cols].reshape(n_rows, step)
        act[...] += jnp.dot(left, block[:, 2 * hidden :], preferred_element_type=jnp.float32)
        return carry

    lax.fori_loop(0, width // step, project, 0)

    pre_gate = pre[:, :hidden]
    pre_up = pre[:, hidden:]
    grad_act = act[:, :hidden]
    sigmoid_value = jax.nn.sigmoid(pre_gate)
    silu_value = pre_gate * sigmoid_value
    slope = sigmoid_value * (1.0 + pre_gate * (1.0 - sigmoid_value))
    pair[...] = jnp.concatenate(
        [grad_act * pre_up * slope, grad_act * silu_value], axis=1
    ).astype(jnp.bfloat16)
    active[...] = jnp.concatenate(
        [silu_value * pre_up, jnp.zeros((n_rows, act.shape[1] - hidden), jnp.float32)], axis=1
    ).astype(jnp.bfloat16)

    def back_project(c, carry):
        cols = pl.ds(pl.multiple_of(c * step, step), step)
        block = weights[pl.ds(c * blocks, blocks)].reshape(step, lanes)
        part = lax.dot_general(
            pair[...], block[:, : 2 * hidden], LAST, preferred_element_type=jnp.float32
        )
        parts[:, :, cols] = part.astype(jnp.bfloat16).reshape(RING, CAP, step)
        return carry

    lax.fori_loop(0, width // step, back_project, 0)

    def left_chain(k):
        return copy_to(
            parts.at[RING - k],
            from_right.at[k - 1],
            back_left.at[k],
            right_recv.at[k - 1],
            plane(-1),
        )

    def left_exit(k):
        to = k // 5
        return copy_to(
            parts.at[RING - k],
            finals.at[to],
            back_left.at[k],
            final_recv.at[to],
            plane(-k),
        )

    def right_chain(k):
        return copy_to(
            parts.at[k],
            from_left.at[k - 1],
            back_right.at[k],
            left_recv.at[k - 1],
            plane(1),
        )

    def right_exit(k):
        to = 2 - k // 5
        return copy_to(
            parts.at[k],
            finals.at[to],
            back_right.at[k],
            final_recv.at[to],
            plane(k),
        )

    def got_right(k):
        copy_to(
            from_right.at[k], from_right.at[k], back_left.at[0], right_recv.at[k], plane(1)
        ).wait_recv()

    def got_left(k):
        copy_to(
            from_left.at[k], from_left.at[k], back_right.at[0], left_recv.at[k], plane(-1)
        ).wait_recv()

    def add_bf16(one, two):
        return (one.astype(jnp.float32) + two.astype(jnp.float32)).astype(jnp.bfloat16)

    @pl.when(member == SPLIT - 1)
    def _():
        def start(i, carry):
            left_chain(REACH - i).start()
            return carry

        lax.fori_loop(0, REACH, start, 0)

    @pl.when(member == 0)
    def _():
        def start(i, carry):
            right_chain(REACH - i).start()
            return carry

        lax.fori_loop(0, REACH, start, 0)

    def weight_grads(c, carry):
        first = lax.rem(c * blocks + (1 - core) * half, n_dp)
        cols = pl.ds(pl.multiple_of(first * depth, step), step)
        left = rows_in[:, :, cols].reshape(n_rows, step)
        one = lax.dot_general(left, pair[...], FIRST, preferred_element_type=jnp.float32)
        left = rows_grad[:, :, cols].reshape(n_rows, step)
        two = lax.dot_general(left, active[...], FIRST, preferred_element_type=jnp.float32)
        grads[pl.ds(first, blocks)] = (
            jnp.concatenate([one, two], axis=1).astype(jnp.bfloat16).reshape(blocks, depth, lanes)
        )
        return carry

    chunks = width // step
    lax.fori_loop(0, chunks // 2, weight_grads, 0)
    to_sibling = copy_to(
        grads.at[pl.ds((1 - core) * half, half)],
        sibling_grads,
        sibling_send,
        sibling_recv,
        (sibling, z),
    )
    to_sibling.start()
    lax.fori_loop(chunks // 2, chunks, weight_grads, 0)

    def pass_sums(i, carry):
        k = REACH - i

        @pl.when((k <= member + FAR) & (member < SPLIT - 1))
        def _():
            got_right(k)
            parts[RING - k] = add_bf16(parts[RING - k], from_right[k])

            @pl.when(member > 0)
            def _():
                left_chain(k).start()

            @pl.when(member == 0)
            def _():
                left_exit(k).start()

        @pl.when((k <= REACH - member) & (member > 0))
        def _():
            got_left(k)
            parts[k] = add_bf16(parts[k], from_left[k])

            @pl.when(member < SPLIT - 1)
            def _():
                right_chain(k).start()

            @pl.when(member == SPLIT - 1)
            def _():
                right_exit(k).start()

        return carry

    lax.fori_loop(0, REACH, pass_sums, 0)

    to_sibling.wait_recv()

    def grad_copy(i):
        return copy_to(
            grads.at[core * half + i],
            grads_in.at[chip],
            grad_send.at[i],
            grad_recv.at[chip],
            (core * half + i, z),
        )

    def send_grads(i, carry):
        to = core * half + i
        summed = add_bf16(grads[to], sibling_grads[i])
        grads[to] = summed

        @pl.when(to != dp)
        def _():
            grad_copy(i).start()

        @pl.when(to == dp)
        def _():
            grads_in[chip] = summed

        return carry

    lax.fori_loop(0, half, send_grads, 0)

    @pl.when(member < SPLIT - 1)
    def _():
        got_right(0)

    @pl.when(member == SPLIT - 1)
    def _():
        from_right[0] = jnp.zeros((CAP, width), jnp.bfloat16)

    @pl.when(member > 0)
    def _():
        got_left(0)

    @pl.when(member == 0)
    def _():
        from_left[0] = jnp.zeros((CAP, width), jnp.bfloat16)

    for i in range(3):
        copy_to(
            finals.at[i], finals.at[i], back_left.at[0], final_recv.at[i], plane(1)
        ).wait_recv()

    own_place = place[group]
    where_from = jnp.concatenate(
        [
            place[lax.rem(group + 1, SPLIT)],
            place[lax.rem(group + 2, SPLIT)],
            place[lax.rem(group + 3, SPLIT)],
            own_place,
            own_place,
            own_place,
        ],
        axis=0,
    )

    def give_back(c, carry):
        cols = pl.ds(pl.multiple_of(c * step, step), step)
        values = jnp.concatenate(
            [
                finals[:, :, cols].reshape(3 * CAP, step),
                parts[0, :, cols],
                from_right[0, :, cols],
                from_left[0, :, cols],
            ],
            axis=0,
        )
        grad_tokens[:, cols] = lax.dot_general(
            where_from, values, FIRST, preferred_element_type=jnp.float32
        ).astype(jnp.bfloat16)
        return carry

    lax.fori_loop(0, width // step, give_back, 0)

    def grads_arrived(i, carry):
        sender = 2 * i + dp // half

        @pl.when(sender != dp)
        def _():
            copy_to(
                grads_in.at[i], grads_in.at[i], grad_send.at[i], grad_recv.at[i], (sibling, z)
            ).wait_recv()

        return carry

    lax.fori_loop(0, half, grads_arrived, 0)
    total = jnp.sum(grads_in[...].astype(jnp.float32), axis=0)
    grad_gate[...] = total[:, :hidden]
    grad_up[...] = total[:, hidden : 2 * hidden]
    grad_down[...] = total[:, 2 * hidden : 3 * hidden]

    for copy in near + far:
        copy.wait_send()

    @pl.when(member < SPLIT - 1)
    def _():
        for copy in own_right:
            copy.wait_send()

    @pl.when(member > 0)
    def _():
        for copy in own_left:
            copy.wait_send()

    def drain(k, carry):
        @pl.when(k <= member + FAR)
        def _():
            left_chain(k).wait_send()

            @pl.when(member < SPLIT - 1)
            def _():
                for h, (_, rows) in enumerate(both):
                    right_pass(k, h, rows).wait_send()

        @pl.when(k <= REACH - member)
        def _():
            right_chain(k).wait_send()

            @pl.when(member > 0)
            def _():
                for h, (_, rows) in enumerate(both):
                    left_pass(k, h, rows).wait_send()

        return carry

    lax.fori_loop(1, REACH + 1, drain, 0)

    def drain_weights(i, carry):
        weight_copy(i).wait_send()
        return carry

    lax.fori_loop(1, n_dp, drain_weights, 0)
    to_sibling.wait_send()

    def drain_grads(i, carry):
        @pl.when(core * half + i != dp)
        def _():
            grad_copy(i).wait_send()

        return carry

    lax.fori_loop(0, half, drain_grads, 0)


def body(n_dp, tokens, cotangent, ids, mask, gates, gate_w, up_w, down_w):
    n_tok, width = tokens.shape
    depth, hidden = gate_w.shape
    lanes = -(-3 * hidden // 128) * 128
    n_rows = RING * CAP
    half = n_dp // 2
    bf16, f32 = jnp.bfloat16, jnp.float32
    vmem = pl.BlockSpec(memory_space=pltpu.VMEM)
    dma = pltpu.SemaphoreType.DMA
    grad_tokens, grad_gate, grad_up, grad_down = pl.pallas_call(
        kernel,
        out_shape=(
            jax.ShapeDtypeStruct((n_tok, width), bf16),
            jax.ShapeDtypeStruct((depth, hidden), f32),
            jax.ShapeDtypeStruct((depth, hidden), f32),
            jax.ShapeDtypeStruct((depth, hidden), f32),
        ),
        in_specs=[vmem] * 8,
        out_specs=[vmem] * 4,
        scratch_shapes=[
            pltpu.VMEM((SPLIT, CAP, n_tok), bf16),
            pltpu.VMEM((SPLIT, CAP, width), bf16),
            pltpu.VMEM((SPLIT, CAP, width), bf16),
            pltpu.VMEM((RING, CAP, width), bf16),
            pltpu.VMEM((RING, CAP, width), bf16),
            pltpu.VMEM((n_dp, depth, lanes), bf16),
            pltpu.VMEM((n_rows, 2 * hidden), f32),
            pltpu.VMEM((n_rows, lanes - 2 * hidden), f32),
            pltpu.VMEM((n_rows, 2 * hidden), bf16),
            pltpu.VMEM((n_rows, lanes - 2 * hidden), bf16),
            pltpu.VMEM((RING, CAP, width), bf16),
            pltpu.VMEM((REACH + 1, CAP, width), bf16),
            pltpu.VMEM((REACH + 1, CAP, width), bf16),
            pltpu.VMEM((3, CAP, width), bf16),
            pltpu.VMEM((n_dp, depth, lanes), bf16),
            pltpu.VMEM((half, depth, lanes), bf16),
            pltpu.VMEM((half, depth, lanes), bf16),
            dma((5, 2)),
            dma((REACH + 1, 2)),
            dma((REACH + 1, 2)),
            dma((RING, 2)),
            dma((n_dp,)),
            dma((n_dp,)),
            dma((REACH + 1,)),
            dma((REACH + 1,)),
            dma((REACH + 1,)),
            dma((REACH + 1,)),
            dma((3,)),
            dma,
            dma,
            dma((half,)),
            dma((half,)),
        ],
        compiler_params=pltpu.CompilerParams(
            collective_id=0, has_side_effects=True, vmem_limit_bytes=48 * 1024 * 1024
        ),
        cost_estimate=pl.CostEstimate(
            flops=16 * n_rows * width * hidden, bytes_accessed=1 << 21, transcendentals=1 << 16
        ),
    )(tokens, cotangent, ids.T, mask.T, gates.T, gate_w, up_w, down_w.T)
    return grad_tokens, grad_gate, grad_up, grad_down.T


def solution(mesh):
    rows = P(("dp", "expert"), None)
    return jax.shard_map(
        functools.partial(body, mesh.shape["dp"]),
        mesh=mesh,
        in_specs=(rows, rows, rows, rows, rows) + (P("dp", "expert"),) * 2 + (P("expert", "dp"),),
        out_specs=(rows, P("dp", "expert"), P("dp", "expert"), P("expert", "dp")),
        check_vma=False,
    )
```

```python
import functools

import jax
import jax.numpy as jnp
from jax import lax
from jax.experimental import pallas as pl
from jax.experimental.pallas import tpu as pltpu
from jax.sharding import PartitionSpec as P

MESH = pl.DeviceIdType.MESH
RING = 16
SPLIT = 4
CHIPS = SPLIT * SPLIT
CAP = 16
STEP = 256
LAST = (((1,), (1,)), ((), ()))
FIRST = (((0,), (0,)), ((), ()))


def copy_to(src, dst, send_sem, recv_sem, device):
    return pltpu.make_async_remote_copy(
        src_ref=src,
        dst_ref=dst,
        send_sem=send_sem,
        recv_sem=recv_sem,
        device_id=device,
        device_id_type=MESH,
    )


def kernel(
    tokens_hbm,
    cotangent_hbm,
    ids_hbm,
    mask_hbm,
    gates_hbm,
    gate_hbm,
    up_hbm,
    down_hbm,
    grad_tokens,
    grad_gate,
    grad_up,
    grad_down,
    tokens,
    cotangent,
    ids,
    mask,
    gates,
    gate_w,
    up_w,
    down_w,
    place,
    rows_in,
    rows_grad,
    out_in,
    out_grad,
    shards,
    weights,
    pre,
    act,
    pair,
    active,
    parts,
    returned,
    sums,
    finals,
    grads,
    sibling_grads,
    grads_in,
    group_sums,
    group_in,
    load_sem,
    entry_send,
    entry_recv,
    side_send,
    side_recv,
    shard_send,
    shard_recv,
    spread_send,
    spread_recv,
    twin_send,
    twin_recv,
    part_send,
    part_recv,
    final_send,
    final_recv,
    sibling_send,
    sibling_recv,
    grad_send,
    grad_recv,
    group_send,
    group_recv,
):
    width = tokens.shape[1]
    depth, hidden = gate_w.shape
    lanes = weights.shape[2]
    n_tok = tokens.shape[0]
    n_rows = RING * CAP
    blocks = STEP // depth
    chunks = width // STEP

    dp = lax.axis_index("dp")
    z = lax.axis_index("expert")
    group = z // SPLIT
    member = lax.rem(z, SPLIT)
    core = lax.rem(dp, 2)
    chip = dp // 2
    x = chip // SPLIT
    y = lax.rem(chip, SPLIT)
    sibling = (dp + 1 - 2 * core, z)

    def plane(offset):
        return (dp, lax.rem(z + offset + RING, RING))

    def at(to_x, to_y):
        return ((lax.rem(to_x + SPLIT, SPLIT) * SPLIT + lax.rem(to_y + SPLIT, SPLIT)) * 2 + core, z)

    up_down = 1 - 2 * core
    to_sides = (at(x + 1, y), at(x - 1, y), at(x, y + up_down))
    from_sides = (at(x - 1, y), at(x + 1, y), at(x, y - up_down))

    loads = [
        pltpu.make_async_copy(source, target, load_sem.at[i])
        for i, (source, target) in enumerate(
            (
                (ids_hbm, ids),
                (mask_hbm, mask),
                (gates_hbm, gates),
                (tokens_hbm, tokens),
                (cotangent_hbm, cotangent),
                (gate_hbm, gate_w),
                (up_hbm, up_w),
                (down_hbm, down_w),
            )
        )
    ]
    for load in loads:
        load.start()

    barrier = pltpu.get_barrier_semaphore()

    def greet_ring(i, carry):
        pl.semaphore_signal(barrier, inc=1, device_id=plane(i), device_id_type=MESH)
        return carry

    def greet_plane(i, carry):
        pl.semaphore_signal(
            barrier, inc=1, device_id=(lax.rem(dp + 2 * i, 2 * CHIPS), z), device_id_type=MESH
        )
        return carry

    lax.fori_loop(1, RING, greet_ring, 0)
    lax.fori_loop(1, CHIPS, greet_plane, 0)
    pl.semaphore_signal(barrier, inc=1, device_id=sibling, device_id_type=MESH)

    for load in loads[:3]:
        load.wait()
    live = mask[...] == 1
    hits, gate_rows = [], []
    for j in range(SPLIT):
        hit = jnp.where((ids[...] == j) & live, 1.0, 0.0)
        hits.append(jnp.sum(hit, axis=0, keepdims=True))
        gate_rows.append(jnp.sum(hit * gates[...], axis=0, keepdims=True))
    hit_rows = jnp.concatenate(hits + [jnp.zeros((CAP - SPLIT, n_tok), jnp.float32)], axis=0)
    earlier = (
        lax.broadcasted_iota(jnp.int32, (n_tok, n_tok), 0)
        < lax.broadcasted_iota(jnp.int32, (n_tok, n_tok), 1)
    )
    rank = jnp.dot(
        hit_rows.astype(jnp.bfloat16),
        jnp.where(earlier, 1.0, 0.0).astype(jnp.bfloat16),
        preferred_element_type=jnp.float32,
    )
    slot = lax.broadcasted_iota(jnp.int32, (CAP, n_tok), 0).astype(jnp.float32)
    slot_gates = []
    for j in range(SPLIT):
        held = jnp.where(
            (jnp.broadcast_to(rank[j : j + 1], (CAP, n_tok)) == slot)
            & (jnp.broadcast_to(hits[j], (CAP, n_tok)) > 0.5),
            1.0,
            0.0,
        )
        place[j] = held.astype(jnp.bfloat16)
        slot_gates.append(jnp.sum(held * gate_rows[j], axis=1, keepdims=True))
    slot_gate = jnp.concatenate(slot_gates, axis=0)
    chosen = place[...].reshape(SPLIT * CAP, n_tok)

    for load in loads[3:]:
        load.wait()

    def fill(c, carry):
        cols = pl.ds(pl.multiple_of(c * STEP, STEP), STEP)
        picked = jnp.dot(chosen, tokens[:, cols], preferred_element_type=jnp.float32)
        out_in[:, :, cols] = picked.astype(jnp.bfloat16).reshape(SPLIT, CAP, STEP)
        picked = jnp.dot(chosen, cotangent[:, cols], preferred_element_type=jnp.float32)
        out_grad[:, :, cols] = (
            (slot_gate * picked).astype(jnp.bfloat16).reshape(SPLIT, CAP, STEP)
        )
        return carry

    lax.fori_loop(0, chunks, fill, 0)
    rows_in[0, 0] = out_in[group]
    rows_grad[0, 0] = out_grad[group]

    packed = jnp.concatenate(
        [
            gate_w[...].astype(jnp.float32),
            up_w[...].astype(jnp.float32),
            down_w[...].astype(jnp.float32),
            jnp.zeros((depth, lanes - 3 * hidden), jnp.float32),
        ],
        axis=1,
    )
    shards[member] = packed.astype(jnp.bfloat16)

    pl.semaphore_wait(barrier, RING - 1 + CHIPS)

    both = ((out_in, rows_in), (out_grad, rows_grad))
    upper = member // 2
    edge = 1 - lax.rem((member + 1) // 2, 2)
    low = (1 - upper) * edge
    high = upper * edge
    entries = []
    for index, offset, place_there, expert in (
        (
            1,
            upper * (8 - member) - (1 - upper) * (member + 5),
            upper * member + (1 - upper) * (3 - member),
            lax.rem(group + 2, SPLIT),
        ),
        (0, 5 - member - low, member + low, lax.rem(group + 1, SPLIT)),
        (2, high - member - 2, 3 - member + high, lax.rem(group + 3, SPLIT)),
    ):
        for h, (source, rows) in enumerate(both):
            entries.append(
                copy_to(
                    source.at[expert],
                    rows.at[0, place_there],
                    entry_send.at[index, h],
                    entry_recv.at[place_there, h],
                    plane(offset),
                )
            )
    for copy in entries:
        copy.start()

    def shard_copy(i):
        return copy_to(
            shards.at[member],
            shards.at[member],
            shard_send.at[i],
            shard_recv.at[member],
            (dp, group * SPLIT + lax.rem(member + i, SPLIT)),
        )

    def spread_copy(part, to_y):
        to_x = lax.rem(part + 2 * to_y, SPLIT)
        return (
            (to_x * SPLIT + to_y) != chip,
            copy_to(
                shards.at[part],
                weights.at[dp],
                spread_send.at[part, to_y],
                spread_recv.at[chip],
                at(to_x, to_y),
            ),
        )

    def spread(i, carry):
        part = lax.rem(member + i, SPLIT)

        @pl.when(i > 0)
        def _():
            copy_to(
                shards.at[part], shards.at[part], shard_send.at[0], shard_recv.at[part], sibling
            ).wait_recv()

        for step in range(SPLIT):
            to_y = lax.rem(y + step, SPLIT)
            elsewhere, copy = spread_copy(part, to_y)
            pl.when(elsewhere)(copy.start)
        return carry

    for i in range(1, SPLIT):
        shard_copy(i).start()

    def side_copy(side, place_here, h):
        rows = both[h][1]
        return copy_to(
            rows.at[0, place_here],
            rows.at[1 + side, place_here],
            side_send.at[side, place_here, h],
            side_recv.at[side, place_here, h],
            to_sides[side],
        )

    def send_sides(place_here):
        for h in range(2):
            for side in range(3):
                side_copy(side, place_here, h).start()

    send_sides(0)
    lax.fori_loop(0, SPLIT, spread, 0)

    my_part = lax.rem(x + 2 * y, SPLIT)
    weights[dp] = shards[my_part]

    def twin_copy(i):
        index = lax.rem(chip + i, CHIPS) * 2 + core
        return copy_to(
            weights.at[index], weights.at[index], twin_send.at[i], twin_recv.at[i], sibling
        )

    twin_copy(0).start()

    def twin(i, carry):
        source = lax.rem(chip + i, CHIPS)
        copy_to(
            weights.at[source * 2 + core],
            weights.at[source * 2 + core],
            twin_send.at[i],
            spread_recv.at[source],
            sibling,
        ).wait_recv()
        twin_copy(i).start()
        return carry

    def pass_sides(place_here, carry):
        for h, (_, rows) in enumerate(both):
            copy_to(
                rows.at[0, place_here],
                rows.at[0, place_here],
                entry_send.at[0, h],
                entry_recv.at[place_here, h],
                sibling,
            ).wait_recv()
            for side in range(3):
                side_copy(side, place_here, h).start()
        return carry

    lax.fori_loop(1, SPLIT, pass_sides, 0)
    lax.fori_loop(1, CHIPS, twin, 0)

    def sides_arrived(place_here, carry):
        for side in range(3):
            for h, (_, rows) in enumerate(both):
                copy_to(
                    rows.at[1 + side, place_here],
                    rows.at[1 + side, place_here],
                    side_send.at[side, place_here, h],
                    side_recv.at[side, place_here, h],
                    sibling,
                ).wait_recv()
        return carry

    lax.fori_loop(0, SPLIT, sides_arrived, 0)

    def twins_arrived(i, carry):
        index = lax.rem(chip + i, CHIPS) * 2 + 1 - core
        copy_to(
            weights.at[index], weights.at[index], twin_send.at[i], twin_recv.at[i], sibling
        ).wait_recv()
        return carry

    lax.fori_loop(0, CHIPS, twins_arrived, 0)

    pre[...] = jnp.zeros_like(pre)
    act[...] = jnp.zeros_like(act)

    def project(c, carry):
        cols = pl.ds(pl.multiple_of(c * STEP, STEP), STEP)
        block = weights[pl.ds(c * blocks, blocks)].reshape(STEP, lanes)
        left = rows_in[:, :, :, cols].reshape(n_rows, STEP)
        pre[...] += jnp.dot(left, block[:, : 2 * hidden], preferred_element_type=jnp.float32)
        left = rows_grad[:, :, :, cols].reshape(n_rows, STEP)
        act[...] += jnp.dot(left, block[:, 2 * hidden :], preferred_element_type=jnp.float32)
        return carry

    lax.fori_loop(0, chunks, project, 0)

    pre_gate = pre[:, :hidden]
    pre_up = pre[:, hidden:]
    grad_act = act[:, :hidden]
    sigmoid_value = jax.nn.sigmoid(pre_gate)
    silu_value = pre_gate * sigmoid_value
    slope = sigmoid_value * (1.0 + pre_gate * (1.0 - sigmoid_value))
    pair[...] = jnp.concatenate(
        [grad_act * pre_up * slope, grad_act * silu_value], axis=1
    ).astype(jnp.bfloat16)
    active[...] = jnp.concatenate(
        [silu_value * pre_up, jnp.zeros((n_rows, act.shape[1] - hidden), jnp.float32)], axis=1
    ).astype(jnp.bfloat16)

    def back_project(c, carry):
        cols = pl.ds(pl.multiple_of(c * STEP, STEP), STEP)
        block = weights[pl.ds(c * blocks, blocks)].reshape(STEP, lanes)
        part = lax.dot_general(
            pair[...], block[:, : 2 * hidden], LAST, preferred_element_type=jnp.float32
        )
        parts[:, :, :, cols] = part.astype(jnp.bfloat16).reshape(SPLIT, SPLIT, CAP, STEP)
        return carry

    lax.fori_loop(0, chunks, back_project, 0)

    def part_copy(side, place_here):
        return copy_to(
            parts.at[1 + side, place_here],
            returned.at[side, place_here],
            part_send.at[side, place_here],
            part_recv.at[side, place_here],
            from_sides[side],
        )

    def send_parts(i, carry):
        for side in range(3):
            part_copy(side, lax.rem(i, SPLIT)).start()
        return carry

    lax.fori_loop(1, SPLIT + 1, send_parts, 0)

    def sibling_copy(i):
        some = pl.ds(i * SPLIT, SPLIT)
        return copy_to(
            grads.at[1 - core, some],
            sibling_grads.at[some],
            sibling_send.at[i],
            sibling_recv.at[i],
            sibling,
        )

    def weight_grads(i, carry):
        for half in range(2):
            c = 2 * i + half
            cols = pl.ds(pl.multiple_of(c * STEP, STEP), STEP)
            left = rows_in[:, :, :, cols].reshape(n_rows, STEP)
            one = lax.dot_general(left, pair[...], FIRST, preferred_element_type=jnp.float32)
            left = rows_grad[:, :, :, cols].reshape(n_rows, STEP)
            two = lax.dot_general(left, active[...], FIRST, preferred_element_type=jnp.float32)
            both_terms = jnp.concatenate([one, two], axis=1).astype(jnp.bfloat16)
            both_terms = both_terms.reshape(blocks, depth, lanes)
            for b in range(blocks):
                grads[b % 2, c * (blocks // 2) + b // 2] = both_terms[b]
        sibling_copy(i).start()
        return carry

    lax.fori_loop(0, SPLIT, weight_grads, 0)

    def sum_parts(place_here):
        for side in range(3):
            copy_to(
                returned.at[side, place_here],
                returned.at[side, place_here],
                part_send.at[side, place_here],
                part_recv.at[side, place_here],
                sibling,
            ).wait_recv()
        total = parts[0, place_here].astype(jnp.float32)
        for side in range(3):
            total += returned[side, place_here].astype(jnp.float32)
        sums[place_here] = total.astype(jnp.bfloat16)

    def final_copy(place_here):
        late = place_here // 2
        distance = edge * ((1 - late) * 4 + late * (8 - place_here)) + (1 - edge) * (5 - place_here)
        to = edge * late + (1 - edge * late) * 2 * upper
        return copy_to(
            sums.at[place_here],
            finals.at[to],
            final_send.at[place_here],
            final_recv.at[to],
            plane((2 * upper - 1) * distance),
        )

    def send_finals(place_here, carry):
        sum_parts(place_here)
        final_copy(place_here).start()
        return carry

    lax.fori_loop(1, SPLIT, send_finals, 0)

    def grad_copy(i):
        to = lax.rem(chip + i, CHIPS)
        return copy_to(
            grads.at[core, to],
            grads_in.at[chip],
            grad_send.at[i],
            grad_recv.at[chip],
            (2 * to + core, z),
        )

    def sibling_arrived(i, carry):
        some = pl.ds(i * SPLIT, SPLIT)
        copy_to(
            sibling_grads.at[some],
            sibling_grads.at[some],
            sibling_send.at[i],
            sibling_recv.at[i],
            sibling,
        ).wait_recv()
        return carry

    lax.fori_loop(0, SPLIT, sibling_arrived, 0)

    def chip_sum(to):
        return (
            grads[core, to].astype(jnp.float32) + sibling_grads[to].astype(jnp.float32)
        ).astype(jnp.bfloat16)

    grads_in[chip] = chip_sum(chip)

    def send_grads(i, carry):
        to = lax.rem(chip + i, CHIPS)
        grads[core, to] = chip_sum(to)
        grad_copy(i).start()
        return carry

    lax.fori_loop(1, CHIPS, send_grads, 0)

    sum_parts(0)

    def finals_arrived(i, carry):
        copy_to(
            finals.at[i], finals.at[i], final_send.at[1], final_recv.at[i], sibling
        ).wait_recv()
        return carry

    lax.fori_loop(0, 3, finals_arrived, 0)
    where_from = jnp.concatenate(
        [
            place[lax.rem(group + 1, SPLIT)],
            place[lax.rem(group + 2, SPLIT)],
            place[lax.rem(group + 3, SPLIT)],
            place[group],
        ],
        axis=0,
    )

    def give_back(c, carry):
        cols = pl.ds(pl.multiple_of(c * STEP, STEP), STEP)
        values = jnp.concatenate(
            [finals[:, :, cols].reshape(3 * CAP, STEP), sums[0, :, cols]], axis=0
        )
        grad_tokens[:, cols] = lax.dot_general(
            where_from, values, FIRST, preferred_element_type=jnp.float32
        ).astype(jnp.bfloat16)
        return carry

    lax.fori_loop(0, chunks, give_back, 0)

    def plane_sum(part):
        total = jnp.zeros((depth, lanes), jnp.float32)
        for from_y in range(SPLIT):
            source = lax.rem(part + 2 * from_y, SPLIT) * SPLIT + from_y

            @pl.when(source != chip)
            def _():
                copy_to(
                    grads_in.at[source],
                    grads_in.at[source],
                    grad_send.at[0],
                    grad_recv.at[source],
                    sibling,
                ).wait_recv()

            total += grads_in[source].astype(jnp.float32)
        return total

    def group_copy(i):
        part = lax.rem(member + i, SPLIT)
        return copy_to(
            group_sums.at[i],
            group_in.at[SPLIT - i],
            group_send.at[i],
            group_recv.at[SPLIT - i],
            (dp, group * SPLIT + part),
        )

    def send_group(i, carry):
        group_sums[i] = plane_sum(lax.rem(member + i, SPLIT)).astype(jnp.bfloat16)
        group_copy(i).start()
        return carry

    lax.fori_loop(1, SPLIT, send_group, 0)
    total = plane_sum(member)
    for i in range(1, SPLIT):
        copy_to(
            group_in.at[i], group_in.at[i], group_send.at[i], group_recv.at[i], sibling
        ).wait_recv()
        total += group_in[i].astype(jnp.float32)
    grad_gate[...] = total[:, :hidden]
    grad_up[...] = total[:, hidden : 2 * hidden]
    grad_down[...] = total[:, 2 * hidden : 3 * hidden]

    for copy in entries:
        copy.wait_send()

    def drain_places(place_here, carry):
        for side in range(3):
            part_copy(side, place_here).wait_send()
            for h in range(2):
                side_copy(side, place_here, h).wait_send()
        return carry

    lax.fori_loop(0, SPLIT, drain_places, 0)

    def drain_spread(part, carry):
        for to_y in range(SPLIT):
            elsewhere, copy = spread_copy(part, to_y)
            pl.when(elsewhere)(copy.wait_send)
        sibling_copy(part).wait_send()
        return carry

    lax.fori_loop(0, SPLIT, drain_spread, 0)

    def drain_some(i, carry):
        shard_copy(i).wait_send()
        final_copy(i).wait_send()
        group_copy(i).wait_send()
        return carry

    lax.fori_loop(1, SPLIT, drain_some, 0)
    twin_copy(0).wait_send()

    def drain_chips(i, carry):
        twin_copy(i).wait_send()
        grad_copy(i).wait_send()
        return carry

    lax.fori_loop(1, CHIPS, drain_chips, 0)


def body(tokens, cotangent, ids, mask, gates, gate_w, up_w, down_w):
    n_tok, width = tokens.shape
    top = ids.shape[1]
    depth, hidden = gate_w.shape
    lanes = -(-3 * hidden // 128) * 128
    n_rows = RING * CAP
    bf16, f32, i32 = jnp.bfloat16, jnp.float32, jnp.int32
    vmem = pl.BlockSpec(memory_space=pltpu.VMEM)
    dma = pltpu.SemaphoreType.DMA
    grad_tokens, grad_gate, grad_up, grad_down = pl.pallas_call(
        kernel,
        out_shape=(
            jax.ShapeDtypeStruct((n_tok, width), bf16),
            jax.ShapeDtypeStruct((depth, hidden), f32),
            jax.ShapeDtypeStruct((depth, hidden), f32),
            jax.ShapeDtypeStruct((depth, hidden), f32),
        ),
        in_specs=[pl.BlockSpec(memory_space=pl.ANY)] * 8,
        out_specs=[vmem] * 4,
        scratch_shapes=[
            pltpu.VMEM((n_tok, width), bf16),
            pltpu.VMEM((n_tok, width), bf16),
            pltpu.VMEM((top, n_tok), i32),
            pltpu.VMEM((top, n_tok), i32),
            pltpu.VMEM((top, n_tok), f32),
            pltpu.VMEM((depth, hidden), bf16),
            pltpu.VMEM((depth, hidden), bf16),
            pltpu.VMEM((depth, hidden), bf16),
            pltpu.VMEM((SPLIT, CAP, n_tok), bf16),
            pltpu.VMEM((SPLIT, SPLIT, CAP, width), bf16),
            pltpu.VMEM((SPLIT, SPLIT, CAP, width), bf16),
            pltpu.VMEM((SPLIT, CAP, width), bf16),
            pltpu.VMEM((SPLIT, CAP, width), bf16),
            pltpu.VMEM((SPLIT, depth, lanes), bf16),
            pltpu.VMEM((2 * CHIPS, depth, lanes), bf16),
            pltpu.VMEM((n_rows, 2 * hidden), f32),
            pltpu.VMEM((n_rows, lanes - 2 * hidden), f32),
            pltpu.VMEM((n_rows, 2 * hidden), bf16),
            pltpu.VMEM((n_rows, lanes - 2 * hidden), bf16),
            pltpu.VMEM((SPLIT, SPLIT, CAP, width), bf16),
            pltpu.VMEM((3, SPLIT, CAP, width), bf16),
            pltpu.VMEM((SPLIT, CAP, width), bf16),
            pltpu.VMEM((3, CAP, width), bf16),
            pltpu.VMEM((2, CHIPS, depth, lanes), bf16),
            pltpu.VMEM((CHIPS, depth, lanes), bf16),
            pltpu.VMEM((CHIPS, depth, lanes), bf16),
            pltpu.VMEM((SPLIT, depth, lanes), bf16),
            pltpu.VMEM((SPLIT, depth, lanes), bf16),
            dma((8,)),
            dma((3, 2)),
            dma((SPLIT, 2)),
            dma((3, SPLIT, 2)),
            dma((3, SPLIT, 2)),
            dma((SPLIT,)),
            dma((SPLIT,)),
            dma((SPLIT, SPLIT)),
            dma((CHIPS,)),
            dma((CHIPS,)),
            dma((CHIPS,)),
            dma((3, SPLIT)),
            dma((3, SPLIT)),
            dma((SPLIT,)),
            dma((3,)),
            dma((SPLIT,)),
            dma((SPLIT,)),
            dma((CHIPS,)),
            dma((CHIPS,)),
            dma((SPLIT,)),
            dma((SPLIT,)),
        ],
        compiler_params=pltpu.CompilerParams(
            collective_id=0, has_side_effects=True, vmem_limit_bytes=48 * 1024 * 1024
        ),
        cost_estimate=pl.CostEstimate(
            flops=16 * n_rows * width * hidden, bytes_accessed=1 << 21, transcendentals=1 << 16
        ),
    )(tokens, cotangent, ids.T, mask.T, gates.T, gate_w, up_w, down_w.T)
    return grad_tokens, grad_gate, grad_up, grad_down.T


def solution(mesh):
    rows = P(("dp", "expert"), None)
    return jax.shard_map(
        body,
        mesh=mesh,
        in_specs=(rows, rows, rows, rows, rows) + (P("dp", "expert"),) * 2 + (P("expert", "dp"),),
        out_specs=(rows, P("dp", "expert"), P("dp", "expert"), P("expert", "dp")),
        check_vma=False,
    )
```

```python
import functools

import jax
import jax.numpy as jnp
from jax import lax
from jax.experimental import pallas as pl
from jax.experimental.pallas import tpu as pltpu
from jax.sharding import PartitionSpec as P

MESH = pl.DeviceIdType.MESH
RING = 16
SPLIT = 4
CHIPS = SPLIT * SPLIT
CAP = 16
STEP = 512
PIECES = 2
LAST = (((1,), (1,)), ((), ()))
FIRST = (((0,), (0,)), ((), ()))


def copy_to(src, dst, send_sem, recv_sem, device):
    return pltpu.make_async_remote_copy(
        src_ref=src,
        dst_ref=dst,
        send_sem=send_sem,
        recv_sem=recv_sem,
        device_id=device,
        device_id_type=MESH,
    )


def beside(left, right):
    both = [left.astype(jnp.float32), right.astype(jnp.float32)]
    return jnp.concatenate(both, axis=-1).astype(jnp.bfloat16)


def kernel(
    tokens_hbm,
    cotangent_hbm,
    ids_hbm,
    mask_hbm,
    gates_hbm,
    gate_hbm,
    up_hbm,
    down_hbm,
    grad_tokens,
    grad_gate,
    grad_up,
    grad_down,
    tokens,
    cotangent,
    ids,
    mask,
    gates,
    gate_w,
    up_w,
    down_w,
    place,
    rows_in,
    rows_grad,
    out_in,
    out_grad,
    shards,
    weights,
    pre,
    act,
    pair,
    active,
    parts,
    returned,
    sums,
    finals,
    grads,
    sibling_grads,
    grads_in,
    group_sums,
    group_in,
    load_sem,
    entry_send,
    entry_recv,
    side_send,
    side_recv,
    shard_send,
    shard_recv,
    spread_send,
    spread_recv,
    twin_send,
    twin_recv,
    part_send,
    part_recv,
    final_send,
    final_recv,
    sibling_send,
    sibling_recv,
    grad_send,
    grad_recv,
    group_send,
    group_recv,
):
    width = tokens.shape[1]
    depth, hidden = gate_w.shape
    tall = weights.shape[1]
    piece = tall // PIECES
    n_tok = tokens.shape[0]
    n_rows = RING * CAP
    blocks = STEP // depth
    chunks = width // STEP

    dp = lax.axis_index("dp")
    z = lax.axis_index("expert")
    group = z // SPLIT
    member = lax.rem(z, SPLIT)
    core = lax.rem(dp, 2)
    chip = dp // 2
    x = chip // SPLIT
    y = lax.rem(chip, SPLIT)
    sibling = (dp + 1 - 2 * core, z)

    def plane(offset):
        return (dp, lax.rem(z + offset + RING, RING))

    def at(to_x, to_y):
        return ((lax.rem(to_x + SPLIT, SPLIT) * SPLIT + lax.rem(to_y + SPLIT, SPLIT)) * 2 + core, z)

    up_down = 1 - 2 * core
    to_sides = (at(x + 1, y), at(x - 1, y), at(x, y + up_down))
    from_sides = (at(x - 1, y), at(x + 1, y), at(x, y - up_down))

    loads = [
        pltpu.make_async_copy(source, target, load_sem.at[i])
        for i, (source, target) in enumerate(
            (
                (ids_hbm, ids),
                (mask_hbm, mask),
                (gates_hbm, gates),
                (tokens_hbm, tokens),
                (cotangent_hbm, cotangent),
                (gate_hbm, gate_w),
                (up_hbm, up_w),
                (down_hbm, down_w),
            )
        )
    ]
    for load in loads:
        load.start()

    barrier = pltpu.get_barrier_semaphore()

    def greet_ring(i, carry):
        pl.semaphore_signal(barrier, inc=1, device_id=plane(i), device_id_type=MESH)
        return carry

    def greet_plane(i, carry):
        pl.semaphore_signal(
            barrier, inc=1, device_id=(lax.rem(dp + 2 * i, 2 * CHIPS), z), device_id_type=MESH
        )
        return carry

    lax.fori_loop(1, RING, greet_ring, 0)
    lax.fori_loop(1, CHIPS, greet_plane, 0)
    pl.semaphore_signal(barrier, inc=1, device_id=sibling, device_id_type=MESH)

    for load in loads[:3]:
        load.wait()
    live = mask[...] == 1
    hits, gate_rows = [], []
    for j in range(SPLIT):
        hit = jnp.where((ids[...] == j) & live, 1.0, 0.0)
        hits.append(jnp.sum(hit, axis=0, keepdims=True))
        gate_rows.append(jnp.sum(hit * gates[...], axis=0, keepdims=True))
    hit_rows = jnp.concatenate(hits + [jnp.zeros((CAP - SPLIT, n_tok), jnp.float32)], axis=0)
    earlier = (
        lax.broadcasted_iota(jnp.int32, (n_tok, n_tok), 0)
        < lax.broadcasted_iota(jnp.int32, (n_tok, n_tok), 1)
    )
    rank = jnp.dot(
        hit_rows.astype(jnp.bfloat16),
        jnp.where(earlier, 1.0, 0.0).astype(jnp.bfloat16),
        preferred_element_type=jnp.float32,
    )
    slot = lax.broadcasted_iota(jnp.int32, (CAP, n_tok), 0).astype(jnp.float32)
    slot_gates = []
    for j in range(SPLIT):
        held = jnp.where(
            (jnp.broadcast_to(rank[j : j + 1], (CAP, n_tok)) == slot)
            & (jnp.broadcast_to(hits[j], (CAP, n_tok)) > 0.5),
            1.0,
            0.0,
        )
        place[j] = held.astype(jnp.bfloat16)
        slot_gates.append(jnp.sum(held * gate_rows[j], axis=1, keepdims=True))
    slot_gate = jnp.concatenate(slot_gates, axis=0)
    chosen = place[...].reshape(SPLIT * CAP, n_tok)

    for load in loads[3:]:
        load.wait()

    def fill(c, carry):
        cols = pl.ds(pl.multiple_of(c * STEP, STEP), STEP)
        picked = jnp.dot(chosen, tokens[:, cols], preferred_element_type=jnp.float32)
        out_in[:, :, cols] = picked.astype(jnp.bfloat16).reshape(SPLIT, CAP, STEP)
        picked = jnp.dot(chosen, cotangent[:, cols], preferred_element_type=jnp.float32)
        out_grad[:, :, cols] = (
            (slot_gate * picked).astype(jnp.bfloat16).reshape(SPLIT, CAP, STEP)
        )
        return carry

    lax.fori_loop(0, chunks, fill, 0)
    rows_in[0, 0] = out_in[group]
    rows_grad[0, 0] = out_grad[group]

    shards[member, :depth] = beside(gate_w[...], up_w[...])
    shards[member, depth:] = beside(down_w[: depth // 2], down_w[depth // 2 :])

    pl.semaphore_wait(barrier, RING - 1 + CHIPS)

    both = ((out_in, rows_in), (out_grad, rows_grad))
    upper = member // 2
    edge = 1 - lax.rem((member + 1) // 2, 2)
    low = (1 - upper) * edge
    high = upper * edge
    entries = []
    for index, offset, place_there, expert in (
        (
            1,
            upper * (8 - member) - (1 - upper) * (member + 5),
            upper * member + (1 - upper) * (3 - member),
            lax.rem(group + 2, SPLIT),
        ),
        (0, 5 - member - low, member + low, lax.rem(group + 1, SPLIT)),
        (2, high - member - 2, 3 - member + high, lax.rem(group + 3, SPLIT)),
    ):
        for h, (source, rows) in enumerate(both):
            entries.append(
                copy_to(
                    source.at[expert],
                    rows.at[0, place_there],
                    entry_send.at[index, h],
                    entry_recv.at[place_there, h],
                    plane(offset),
                )
            )

    def rows_of(h):
        return pl.ds(h * piece, piece)

    def shard_copy(i, h):
        return copy_to(
            shards.at[member, rows_of(h)],
            shards.at[member, rows_of(h)],
            shard_send.at[i, h],
            shard_recv.at[member, h],
            (dp, group * SPLIT + lax.rem(member + i, SPLIT)),
        )

    def spread_copy(part, to_y, h):
        to_x = lax.rem(part + 2 * to_y, SPLIT)
        return (
            (to_x * SPLIT + to_y) != chip,
            copy_to(
                shards.at[part, rows_of(h)],
                weights.at[dp, rows_of(h)],
                spread_send.at[part, to_y, h],
                spread_recv.at[chip, h],
                at(to_x, to_y),
            ),
        )

    def spread(h, i):
        part = lax.rem(member + i, SPLIT)

        @pl.when(i > 0)
        def _():
            some = shards.at[part, rows_of(h)]
            copy_to(
                some, some, shard_send.at[0, h], shard_recv.at[part, h], sibling
            ).wait_recv()

        for step in range(SPLIT):
            to_y = lax.rem(y + step, SPLIT)
            elsewhere, copy = spread_copy(part, to_y, h)
            pl.when(elsewhere)(copy.start)

    def spread_rest(n, carry):
        spread(n // 3, 1 + lax.rem(n, 3))
        return carry

    def spread_own(h, carry):
        spread(h, 0)
        return carry

    for h in range(PIECES):
        for i in range(1, SPLIT):
            shard_copy(i, h).start()
    for copy in entries:
        copy.start()


    def side_copy(side, place_here, h):
        rows = both[h][1]
        return copy_to(
            rows.at[0, place_here],
            rows.at[1 + side, place_here],
            side_send.at[side, place_here, h],
            side_recv.at[side, place_here, h],
            to_sides[side],
        )

    def send_sides(place_here):
        for h in range(2):
            for side in range(3):
                side_copy(side, place_here, h).start()

    send_sides(0)
    lax.fori_loop(0, PIECES, spread_own, 0)
    lax.fori_loop(0, 3 * PIECES, spread_rest, 0)

    my_part = lax.rem(x + 2 * y, SPLIT)
    weights[dp] = shards[my_part]

    def twin_copy(i, h):
        some = weights.at[lax.rem(chip + i, CHIPS) * 2 + core, rows_of(h)]
        return copy_to(some, some, twin_send.at[i, h], twin_recv.at[i, h], sibling)

    for h in range(PIECES):
        twin_copy(0, h).start()

    def twin(h):
        def one(i, carry):
            source = lax.rem(chip + i, CHIPS)
            some = weights.at[source * 2 + core, rows_of(h)]
            copy_to(
                some, some, twin_send.at[i, h], spread_recv.at[source, h], sibling
            ).wait_recv()
            twin_copy(i, h).start()
            return carry

        lax.fori_loop(1, CHIPS, one, 0)

    def pass_sides(place_here, carry):
        for h, (_, rows) in enumerate(both):
            copy_to(
                rows.at[0, place_here],
                rows.at[0, place_here],
                entry_send.at[0, h],
                entry_recv.at[place_here, h],
                sibling,
            ).wait_recv()
            for side in range(3):
                side_copy(side, place_here, h).start()
        return carry

    pass_sides(1, 0)
    twin(0)
    pass_sides(2, 0)
    pass_sides(3, 0)
    twin(1)

    def sides_arrived(place_here, carry):
        for side in range(3):
            for h, (_, rows) in enumerate(both):
                copy_to(
                    rows.at[1 + side, place_here],
                    rows.at[1 + side, place_here],
                    side_send.at[side, place_here, h],
                    side_recv.at[side, place_here, h],
                    sibling,
                ).wait_recv()
        return carry

    lax.fori_loop(0, SPLIT, sides_arrived, 0)

    def twins_arrived(i, carry):
        for h in range(PIECES):
            some = weights.at[lax.rem(chip + i, CHIPS) * 2 + 1 - core, rows_of(h)]
            copy_to(some, some, twin_send.at[i, h], twin_recv.at[i, h], sibling).wait_recv()
        return carry

    lax.fori_loop(0, CHIPS, twins_arrived, 0)

    pre[...] = jnp.zeros_like(pre)
    act[...] = jnp.zeros_like(act)

    def project(c, carry):
        cols = pl.ds(pl.multiple_of(c * STEP, STEP), STEP)
        some = pl.ds(c * blocks, blocks)
        block = weights[some, :depth].reshape(STEP, 2 * hidden)
        left = rows_in[:, :, :, cols].reshape(n_rows, STEP)
        pre[...] += jnp.dot(left, block, preferred_element_type=jnp.float32)
        below = weights[some, depth:]
        block = jnp.concatenate([below[:, :, :hidden], below[:, :, hidden:]], axis=1)
        left = rows_grad[:, :, :, cols].reshape(n_rows, STEP)
        act[...] += jnp.dot(
            left, block.reshape(STEP, hidden), preferred_element_type=jnp.float32
        )
        return carry

    lax.fori_loop(0, chunks, project, 0)

    pre_gate = pre[:, :hidden]
    pre_up = pre[:, hidden:]
    grad_act = act[...]
    sigmoid_value = jax.nn.sigmoid(pre_gate)
    silu_value = pre_gate * sigmoid_value
    slope = sigmoid_value * (1.0 + pre_gate * (1.0 - sigmoid_value))
    pair[...] = jnp.concatenate(
        [grad_act * pre_up * slope, grad_act * silu_value], axis=1
    ).astype(jnp.bfloat16)
    active[...] = (silu_value * pre_up).astype(jnp.bfloat16)

    def back_project(c, carry):
        cols = pl.ds(pl.multiple_of(c * STEP, STEP), STEP)
        block = weights[pl.ds(c * blocks, blocks), :depth].reshape(STEP, 2 * hidden)
        part = lax.dot_general(pair[...], block, LAST, preferred_element_type=jnp.float32)
        parts[:, :, :, cols] = part.astype(jnp.bfloat16).reshape(SPLIT, SPLIT, CAP, STEP)
        return carry

    lax.fori_loop(0, chunks, back_project, 0)

    def part_copy(side, place_here):
        return copy_to(
            parts.at[1 + side, place_here],
            returned.at[side, place_here],
            part_send.at[side, place_here],
            part_recv.at[side, place_here],
            from_sides[side],
        )

    def send_parts(i, carry):
        for side in range(3):
            part_copy(side, lax.rem(i, SPLIT)).start()
        return carry

    lax.fori_loop(1, SPLIT + 1, send_parts, 0)

    def sibling_copy(i):
        some = pl.ds(i * SPLIT, SPLIT)
        return copy_to(
            grads.at[1 - core, some],
            sibling_grads.at[some],
            sibling_send.at[i],
            sibling_recv.at[i],
            sibling,
        )

    def weight_grads(i, carry):
        for half in range(1):
            c = i + half
            cols = pl.ds(pl.multiple_of(c * STEP, STEP), STEP)
            left = rows_in[:, :, :, cols].reshape(n_rows, STEP)
            one = lax.dot_general(left, pair[...], FIRST, preferred_element_type=jnp.float32)
            left = rows_grad[:, :, :, cols].reshape(n_rows, STEP)
            two = lax.dot_general(left, active[...], FIRST, preferred_element_type=jnp.float32)
            one = one.astype(jnp.bfloat16).reshape(blocks, depth, 2 * hidden)
            two = two.reshape(blocks, 2, depth // 2, hidden)
            for b in range(blocks):
                to = c * (blocks // 2) + b // 2
                grads[b % 2, to, :depth] = one[b]
                grads[b % 2, to, depth:] = beside(two[b, 0], two[b, 1])
        sibling_copy(i).start()
        return carry

    lax.fori_loop(0, SPLIT, weight_grads, 0)

    def sum_parts(place_here):
        for side in range(3):
            copy_to(
                returned.at[side, place_here],
                returned.at[side, place_here],
                part_send.at[side, place_here],
                part_recv.at[side, place_here],
                sibling,
            ).wait_recv()
        total = parts[0, place_here].astype(jnp.float32)
        for side in range(3):
            total += returned[side, place_here].astype(jnp.float32)
        sums[place_here] = total.astype(jnp.bfloat16)

    def final_copy(place_here):
        late = place_here // 2
        distance = edge * ((1 - late) * 4 + late * (8 - place_here)) + (1 - edge) * (5 - place_here)
        to = edge * late + (1 - edge * late) * 2 * upper
        return copy_to(
            sums.at[place_here],
            finals.at[to],
            final_send.at[place_here],
            final_recv.at[to],
            plane((2 * upper - 1) * distance),
        )

    def send_finals(place_here, carry):
        sum_parts(place_here)
        final_copy(place_here).start()
        return carry

    lax.fori_loop(1, SPLIT, send_finals, 0)

    def grad_copy(i, h):
        to = lax.rem(chip + i, CHIPS)
        return copy_to(
            grads.at[core, to, rows_of(h)],
            grads_in.at[chip, rows_of(h)],
            grad_send.at[i, h],
            grad_recv.at[chip, h],
            (2 * to + core, z),
        )

    def sibling_arrived(i, carry):
        some = pl.ds(i * SPLIT, SPLIT)
        copy_to(
            sibling_grads.at[some],
            sibling_grads.at[some],
            sibling_send.at[i],
            sibling_recv.at[i],
            sibling,
        ).wait_recv()
        return carry

    lax.fori_loop(0, SPLIT, sibling_arrived, 0)

    def chip_sum(to):
        return (
            grads[core, to].astype(jnp.float32) + sibling_grads[to].astype(jnp.float32)
        ).astype(jnp.bfloat16)

    grads_in[chip] = chip_sum(chip)

    def send_grads(i, carry):
        to = lax.rem(chip + i, CHIPS)
        grads[core, to] = chip_sum(to)
        grad_copy(i, 0).start()
        return carry

    lax.fori_loop(1, CHIPS, send_grads, 0)

    def send_later(i, carry):
        for h in range(1, PIECES):
            grad_copy(i, h).start()
        return carry

    lax.fori_loop(1, CHIPS, send_later, 0)

    sum_parts(0)

    def finals_arrived(i, carry):
        copy_to(
            finals.at[i], finals.at[i], final_send.at[1], final_recv.at[i], sibling
        ).wait_recv()
        return carry

    lax.fori_loop(0, 3, finals_arrived, 0)
    where_from = jnp.concatenate(
        [
            place[lax.rem(group + 1, SPLIT)],
            place[lax.rem(group + 2, SPLIT)],
            place[lax.rem(group + 3, SPLIT)],
            place[group],
        ],
        axis=0,
    )

    def give_back(c, carry):
        cols = pl.ds(pl.multiple_of(c * STEP, STEP), STEP)
        values = jnp.concatenate(
            [finals[:, :, cols].reshape(3 * CAP, STEP), sums[0, :, cols]], axis=0
        )
        grad_tokens[:, cols] = lax.dot_general(
            where_from, values, FIRST, preferred_element_type=jnp.float32
        ).astype(jnp.bfloat16)
        return carry

    lax.fori_loop(0, chunks, give_back, 0)

    def plane_sum(part, h):
        total = jnp.zeros((piece, 2 * hidden), jnp.float32)
        for from_y in range(SPLIT):
            source = lax.rem(part + 2 * from_y, SPLIT) * SPLIT + from_y

            @pl.when(source != chip)
            def _():
                some = grads_in.at[source, rows_of(h)]
                copy_to(some, some, grad_send.at[0, h], grad_recv.at[source, h], sibling).wait_recv()

            total += grads_in[source, rows_of(h)].astype(jnp.float32)
        return total

    def group_copy(i, h):
        part = lax.rem(member + i, SPLIT)
        return copy_to(
            group_sums.at[i, rows_of(h)],
            group_in.at[SPLIT - i, rows_of(h)],
            group_send.at[i, h],
            group_recv.at[SPLIT - i, h],
            (dp, group * SPLIT + part),
        )

    def send_group(n, carry):
        h, i = n // 3, 1 + lax.rem(n, 3)
        group_sums[i, rows_of(h)] = plane_sum(lax.rem(member + i, SPLIT), h).astype(jnp.bfloat16)
        group_copy(i, h).start()
        return carry

    lax.fori_loop(0, 3 * PIECES, send_group, 0)
    total = jnp.concatenate([plane_sum(member, h) for h in range(PIECES)], axis=0)
    for i in range(1, SPLIT):
        for h in range(PIECES):
            some = group_in.at[i, rows_of(h)]
            copy_to(some, some, group_send.at[i, h], group_recv.at[i, h], sibling).wait_recv()
        total += group_in[i].astype(jnp.float32)
    grad_gate[...] = total[:depth, :hidden]
    grad_up[...] = total[:depth, hidden:]
    grad_down[: depth // 2] = total[depth:, :hidden]
    grad_down[depth // 2 :] = total[depth:, hidden:]

    for copy in entries:
        copy.wait_send()

    def drain_places(place_here, carry):
        for side in range(3):
            part_copy(side, place_here).wait_send()
            for h in range(2):
                side_copy(side, place_here, h).wait_send()
        return carry

    lax.fori_loop(0, SPLIT, drain_places, 0)

    def drain_spread(part, carry):
        for to_y in range(SPLIT):
            for h in range(PIECES):
                elsewhere, copy = spread_copy(part, to_y, h)
                pl.when(elsewhere)(copy.wait_send)
        sibling_copy(part).wait_send()
        return carry

    lax.fori_loop(0, SPLIT, drain_spread, 0)

    def drain_some(i, carry):
        final_copy(i).wait_send()
        for h in range(PIECES):
            shard_copy(i, h).wait_send()
            group_copy(i, h).wait_send()
        return carry

    lax.fori_loop(1, SPLIT, drain_some, 0)
    for h in range(PIECES):
        twin_copy(0, h).wait_send()

    def drain_chips(i, carry):
        for h in range(PIECES):
            twin_copy(i, h).wait_send()
            grad_copy(i, h).wait_send()
        return carry

    lax.fori_loop(1, CHIPS, drain_chips, 0)


def body(tokens, cotangent, ids, mask, gates, gate_w, up_w, down_w):
    n_tok, width = tokens.shape
    top = ids.shape[1]
    depth, hidden = gate_w.shape
    tall = depth * 3 // 2
    n_rows = RING * CAP
    bf16, f32, i32 = jnp.bfloat16, jnp.float32, jnp.int32
    vmem = pl.BlockSpec(memory_space=pltpu.VMEM)
    dma = pltpu.SemaphoreType.DMA
    grad_tokens, grad_gate, grad_up, grad_down = pl.pallas_call(
        kernel,
        out_shape=(
            jax.ShapeDtypeStruct((n_tok, width), bf16),
            jax.ShapeDtypeStruct((depth, hidden), f32),
            jax.ShapeDtypeStruct((depth, hidden), f32),
            jax.ShapeDtypeStruct((depth, hidden), f32),
        ),
        in_specs=[pl.BlockSpec(memory_space=pltpu.HBM)] * 8,
        out_specs=[vmem] * 4,
        scratch_shapes=[
            pltpu.VMEM((n_tok, width), bf16),
            pltpu.VMEM((n_tok, width), bf16),
            pltpu.VMEM((top, n_tok), i32),
            pltpu.VMEM((top, n_tok), i32),
            pltpu.VMEM((top, n_tok), f32),
            pltpu.VMEM((depth, hidden), bf16),
            pltpu.VMEM((depth, hidden), bf16),
            pltpu.VMEM((depth, hidden), bf16),
            pltpu.VMEM((SPLIT, CAP, n_tok), bf16),
            pltpu.VMEM((SPLIT, SPLIT, CAP, width), bf16),
            pltpu.VMEM((SPLIT, SPLIT, CAP, width), bf16),
            pltpu.VMEM((SPLIT, CAP, width), bf16),
            pltpu.VMEM((SPLIT, CAP, width), bf16),
            pltpu.VMEM((SPLIT, tall, 2 * hidden), bf16),
            pltpu.VMEM((2 * CHIPS, tall, 2 * hidden), bf16),
            pltpu.VMEM((n_rows, 2 * hidden), f32),
            pltpu.VMEM((n_rows, hidden), f32),
            pltpu.VMEM((n_rows, 2 * hidden), bf16),
            pltpu.VMEM((n_rows, hidden), bf16),
            pltpu.VMEM((SPLIT, SPLIT, CAP, width), bf16),
            pltpu.VMEM((3, SPLIT, CAP, width), bf16),
            pltpu.VMEM((SPLIT, CAP, width), bf16),
            pltpu.VMEM((3, CAP, width), bf16),
            pltpu.VMEM((2, CHIPS, tall, 2 * hidden), bf16),
            pltpu.VMEM((CHIPS, tall, 2 * hidden), bf16),
            pltpu.VMEM((CHIPS, tall, 2 * hidden), bf16),
            pltpu.VMEM((SPLIT, tall, 2 * hidden), bf16),
            pltpu.VMEM((SPLIT, tall, 2 * hidden), bf16),
            dma((8,)),
            dma((3, 2)),
            dma((SPLIT, 2)),
            dma((3, SPLIT, 2)),
            dma((3, SPLIT, 2)),
            dma((SPLIT, PIECES)),
            dma((SPLIT, PIECES)),
            dma((SPLIT, SPLIT, PIECES)),
            dma((CHIPS, PIECES)),
            dma((CHIPS, PIECES)),
            dma((CHIPS, PIECES)),
            dma((3, SPLIT)),
            dma((3, SPLIT)),
            dma((SPLIT,)),
            dma((3,)),
            dma((SPLIT,)),
            dma((SPLIT,)),
            dma((CHIPS, PIECES)),
            dma((CHIPS, PIECES)),
            dma((SPLIT, PIECES)),
            dma((SPLIT, PIECES)),
        ],
        compiler_params=pltpu.CompilerParams(
            collective_id=0, has_side_effects=True, vmem_limit_bytes=64 * 1024 * 1024 - 131072
        ),
        cost_estimate=pl.CostEstimate(
            flops=16 * n_rows * width * hidden, bytes_accessed=1 << 21, transcendentals=1 << 16
        ),
    )(tokens, cotangent, ids.T, mask.T, gates.T, gate_w, up_w, down_w.T)
    return grad_tokens, grad_gate, grad_up, grad_down.T


def solution(mesh):
    rows = P(("dp", "expert"), None)
    return jax.shard_map(
        body,
        mesh=mesh,
        in_specs=(rows, rows, rows, rows, rows) + (P("dp", "expert"),) * 2 + (P("expert", "dp"),),
        out_specs=(rows, P("dp", "expert"), P("dp", "expert"), P("expert", "dp")),
        check_vma=False,
    )
```

```python
import functools

import jax
import jax.numpy as jnp
from jax import lax
from jax.experimental import pallas as pl
from jax.experimental.pallas import tpu as pltpu
from jax.sharding import PartitionSpec as P

MESH = pl.DeviceIdType.MESH
RING = 16
SPLIT = 4
CHIPS = SPLIT * SPLIT
CAP = 16
STEP = 512
VMEM_BYTES = 64 * 1024 * 1024 - 131072
PIECES = 2
LAST = (((1,), (1,)), ((), ()))
FIRST = (((0,), (0,)), ((), ()))


def copy_to(src, dst, send_sem, recv_sem, device):
    return pltpu.make_async_remote_copy(
        src_ref=src,
        dst_ref=dst,
        send_sem=send_sem,
        recv_sem=recv_sem,
        device_id=device,
        device_id_type=MESH,
    )


def beside(left, right):
    both = [left.astype(jnp.float32), right.astype(jnp.float32)]
    return jnp.concatenate(both, axis=-1).astype(jnp.bfloat16)


def kernel(
    tokens_hbm,
    cotangent_hbm,
    ids_hbm,
    mask_hbm,
    gates_hbm,
    gate_hbm,
    up_hbm,
    down_hbm,
    grad_tokens,
    grad_gate,
    grad_up,
    grad_down,
    tokens,
    cotangent,
    ids,
    mask,
    gates,
    gate_w,
    up_w,
    down_w,
    place,
    rows_in,
    rows_grad,
    out_in,
    out_grad,
    shards,
    weights,
    pre,
    act,
    pair,
    active,
    parts,
    returned,
    sums,
    finals,
    grads,
    sibling_grads,
    grads_in,
    group_sums,
    group_in,
    load_sem,
    entry_send,
    entry_recv,
    side_send,
    side_recv,
    shard_send,
    shard_recv,
    spread_send,
    spread_recv,
    twin_send,
    twin_recv,
    part_send,
    part_recv,
    final_send,
    final_recv,
    sibling_send,
    sibling_recv,
    grad_send,
    grad_recv,
    group_send,
    group_recv,
):
    width = tokens.shape[1]
    depth, hidden = gate_w.shape
    tall = weights.shape[1]
    piece = tall // PIECES
    n_tok = tokens.shape[0]
    n_rows = RING * CAP
    blocks = STEP // depth
    chunks = width // STEP

    dp = lax.axis_index("dp")
    z = lax.axis_index("expert")
    group = z // SPLIT
    member = lax.rem(z, SPLIT)
    core = lax.rem(dp, 2)
    chip = dp // 2
    x = chip // SPLIT
    y = lax.rem(chip, SPLIT)
    sibling = (dp + 1 - 2 * core, z)

    def plane(offset):
        return (dp, lax.rem(z + offset + RING, RING))

    def at(to_x, to_y):
        return ((lax.rem(to_x + SPLIT, SPLIT) * SPLIT + lax.rem(to_y + SPLIT, SPLIT)) * 2 + core, z)

    up_down = 1 - 2 * core
    to_sides = (at(x + 1, y), at(x - 1, y), at(x, y + up_down))
    from_sides = (at(x - 1, y), at(x + 1, y), at(x, y - up_down))

    loads = [
        pltpu.make_async_copy(source, target, load_sem.at[i])
        for i, (source, target) in enumerate(
            (
                (ids_hbm, ids),
                (mask_hbm, mask),
                (gates_hbm, gates),
                (tokens_hbm, tokens),
                (cotangent_hbm, cotangent),
                (gate_hbm, gate_w),
                (up_hbm, up_w),
                (down_hbm, down_w),
            )
        )
    ]
    for load in loads:
        load.start()

    barrier = pltpu.get_barrier_semaphore()

    def greet_ring(i, carry):
        pl.semaphore_signal(barrier, inc=1, device_id=plane(i), device_id_type=MESH)
        return carry

    def greet_plane(i, carry):
        pl.semaphore_signal(
            barrier, inc=1, device_id=(lax.rem(dp + 2 * i, 2 * CHIPS), z), device_id_type=MESH
        )
        return carry

    lax.fori_loop(1, RING, greet_ring, 0)
    lax.fori_loop(1, CHIPS, greet_plane, 0)
    pl.semaphore_signal(barrier, inc=1, device_id=sibling, device_id_type=MESH)

    for load in loads[:3]:
        load.wait()
    live = mask[...] == 1
    hits, gate_rows = [], []
    for j in range(SPLIT):
        hit = jnp.where((ids[...] == j) & live, 1.0, 0.0)
        hits.append(jnp.sum(hit, axis=0, keepdims=True))
        gate_rows.append(jnp.sum(hit * gates[...], axis=0, keepdims=True))
    hit_rows = jnp.concatenate(hits + [jnp.zeros((CAP - SPLIT, n_tok), jnp.float32)], axis=0)
    earlier = (
        lax.broadcasted_iota(jnp.int32, (n_tok, n_tok), 0)
        < lax.broadcasted_iota(jnp.int32, (n_tok, n_tok), 1)
    )
    rank = jnp.dot(
        hit_rows.astype(jnp.bfloat16),
        jnp.where(earlier, 1.0, 0.0).astype(jnp.bfloat16),
        preferred_element_type=jnp.float32,
    )
    slot = lax.broadcasted_iota(jnp.int32, (CAP, n_tok), 0).astype(jnp.float32)
    slot_gates = []
    for j in range(SPLIT):
        held = jnp.where(
            (jnp.broadcast_to(rank[j : j + 1], (CAP, n_tok)) == slot)
            & (jnp.broadcast_to(hits[j], (CAP, n_tok)) > 0.5),
            1.0,
            0.0,
        )
        place[j] = held.astype(jnp.bfloat16)
        slot_gates.append(jnp.sum(held * gate_rows[j], axis=1, keepdims=True))
    slot_gate = jnp.concatenate(slot_gates, axis=0)
    chosen = place[...].reshape(SPLIT * CAP, n_tok)

    for load in loads[3:]:
        load.wait()

    def fill(c, carry):
        cols = pl.ds(pl.multiple_of(c * STEP, STEP), STEP)
        picked = jnp.dot(chosen, tokens[:, cols], preferred_element_type=jnp.float32)
        out_in[:, :, cols] = picked.astype(jnp.bfloat16).reshape(SPLIT, CAP, STEP)
        picked = jnp.dot(chosen, cotangent[:, cols], preferred_element_type=jnp.float32)
        out_grad[:, :, cols] = (
            (slot_gate * picked).astype(jnp.bfloat16).reshape(SPLIT, CAP, STEP)
        )
        return carry

    lax.fori_loop(0, chunks, fill, 0)
    rows_in[0, 0] = out_in[group]
    rows_grad[0, 0] = out_grad[group]

    shards[member, :depth] = beside(gate_w[...], up_w[...])
    shards[member, depth:] = beside(down_w[: depth // 2], down_w[depth // 2 :])

    pl.semaphore_wait(barrier, RING - 1 + CHIPS)

    both = ((out_in, rows_in), (out_grad, rows_grad))
    upper = member // 2
    edge = 1 - lax.rem((member + 1) // 2, 2)
    low = (1 - upper) * edge
    high = upper * edge
    entries = []
    for index, offset, place_there, expert in (
        (
            1,
            upper * (8 - member) - (1 - upper) * (member + 5),
            upper * member + (1 - upper) * (3 - member),
            lax.rem(group + 2, SPLIT),
        ),
        (0, 5 - member - low, member + low, lax.rem(group + 1, SPLIT)),
        (2, high - member - 2, 3 - member + high, lax.rem(group + 3, SPLIT)),
    ):
        for h, (source, rows) in enumerate(both):
            entries.append(
                copy_to(
                    source.at[expert],
                    rows.at[0, place_there],
                    entry_send.at[index, h],
                    entry_recv.at[place_there, h],
                    plane(offset),
                )
            )

    def rows_of(h):
        return pl.ds(h * piece, piece)

    def shard_copy(i, h):
        return copy_to(
            shards.at[member, rows_of(h)],
            shards.at[member, rows_of(h)],
            shard_send.at[i, h],
            shard_recv.at[member, h],
            (dp, group * SPLIT + lax.rem(member + i, SPLIT)),
        )

    def spread_copy(part, to_y, h):
        to_x = lax.rem(part + 2 * to_y, SPLIT)
        return (
            (to_x * SPLIT + to_y) != chip,
            copy_to(
                shards.at[part, rows_of(h)],
                weights.at[dp, rows_of(h)],
                spread_send.at[part, to_y, h],
                spread_recv.at[chip, h],
                at(to_x, to_y),
            ),
        )

    def spread(h, i):
        part = lax.rem(member + i, SPLIT)

        @pl.when(i > 0)
        def _():
            some = shards.at[part, rows_of(h)]
            copy_to(
                some, some, shard_send.at[0, h], shard_recv.at[part, h], sibling
            ).wait_recv()

        for step in range(SPLIT):
            to_y = lax.rem(y + step, SPLIT)
            elsewhere, copy = spread_copy(part, to_y, h)
            pl.when(elsewhere)(copy.start)

    def spread_rest(n, carry):
        spread(n // 3, 1 + lax.rem(n, 3))
        return carry

    def spread_own(h, carry):
        spread(h, 0)
        return carry

    for h in range(PIECES):
        for i in range(1, SPLIT):
            shard_copy(i, h).start()
    for copy in entries:
        copy.start()


    def side_copy(side, place_here, h):
        rows = both[h][1]
        return copy_to(
            rows.at[0, place_here],
            rows.at[1 + side, place_here],
            side_send.at[side, place_here, h],
            side_recv.at[side, place_here, h],
            to_sides[side],
        )

    def send_sides(place_here):
        for h in range(2):
            for side in range(3):
                side_copy(side, place_here, h).start()

    send_sides(0)
    lax.fori_loop(0, PIECES, spread_own, 0)
    lax.fori_loop(0, 3 * PIECES, spread_rest, 0)

    my_part = lax.rem(x + 2 * y, SPLIT)
    weights[dp] = shards[my_part]

    def twin_copy(i, h):
        some = weights.at[lax.rem(chip + i, CHIPS) * 2 + core, rows_of(h)]
        return copy_to(some, some, twin_send.at[i, h], twin_recv.at[i, h], sibling)

    for h in range(PIECES):
        twin_copy(0, h).start()

    def twin(h):
        def one(i, carry):
            source = lax.rem(chip + i, CHIPS)
            some = weights.at[source * 2 + core, rows_of(h)]
            copy_to(
                some, some, twin_send.at[i, h], spread_recv.at[source, h], sibling
            ).wait_recv()
            twin_copy(i, h).start()
            return carry

        lax.fori_loop(1, CHIPS, one, 0)

    def pass_sides(place_here, carry):
        for h, (_, rows) in enumerate(both):
            copy_to(
                rows.at[0, place_here],
                rows.at[0, place_here],
                entry_send.at[0, h],
                entry_recv.at[place_here, h],
                sibling,
            ).wait_recv()
            for side in range(3):
                side_copy(side, place_here, h).start()
        return carry

    pass_sides(1, 0)
    twin(0)
    pass_sides(2, 0)
    pass_sides(3, 0)
    twin(1)

    def sides_arrived(place_here, carry):
        for side in range(3):
            for h, (_, rows) in enumerate(both):
                copy_to(
                    rows.at[1 + side, place_here],
                    rows.at[1 + side, place_here],
                    side_send.at[side, place_here, h],
                    side_recv.at[side, place_here, h],
                    sibling,
                ).wait_recv()
        return carry

    lax.fori_loop(0, SPLIT, sides_arrived, 0)

    def twins_arrived(i, carry):
        for h in range(PIECES):
            some = weights.at[lax.rem(chip + i, CHIPS) * 2 + 1 - core, rows_of(h)]
            copy_to(some, some, twin_send.at[i, h], twin_recv.at[i, h], sibling).wait_recv()
        return carry

    lax.fori_loop(0, CHIPS, twins_arrived, 0)

    pre[...] = jnp.zeros_like(pre)
    act[...] = jnp.zeros_like(act)

    def project(c, carry):
        cols = pl.ds(pl.multiple_of(c * STEP, STEP), STEP)
        some = pl.ds(c * blocks, blocks)
        block = weights[some, :depth].reshape(STEP, 2 * hidden)
        left = rows_in[:, :, :, cols].reshape(n_rows, STEP)
        pre[...] += jnp.dot(left, block, preferred_element_type=jnp.float32)
        below = weights[some, depth:]
        block = jnp.concatenate([below[:, :, :hidden], below[:, :, hidden:]], axis=1)
        left = rows_grad[:, :, :, cols].reshape(n_rows, STEP)
        act[...] += jnp.dot(
            left, block.reshape(STEP, hidden), preferred_element_type=jnp.float32
        )
        return carry

    lax.fori_loop(0, chunks, project, 0, unroll=True)

    pre_gate = pre[:, :hidden]
    pre_up = pre[:, hidden:]
    grad_act = act[...]
    sigmoid_value = jax.nn.sigmoid(pre_gate)
    silu_value = pre_gate * sigmoid_value
    slope = sigmoid_value * (1.0 + pre_gate * (1.0 - sigmoid_value))
    pair[...] = jnp.concatenate(
        [grad_act * pre_up * slope, grad_act * silu_value], axis=1
    ).astype(jnp.bfloat16)
    active[...] = (silu_value * pre_up).astype(jnp.bfloat16)

    def back_project(c, carry):
        cols = pl.ds(pl.multiple_of(c * STEP, STEP), STEP)
        block = weights[pl.ds(c * blocks, blocks), :depth].reshape(STEP, 2 * hidden)
        part = lax.dot_general(pair[...], block, LAST, preferred_element_type=jnp.float32)
        parts[:, :, :, cols] = part.astype(jnp.bfloat16).reshape(SPLIT, SPLIT, CAP, STEP)
        return carry

    lax.fori_loop(0, chunks, back_project, 0, unroll=True)

    def part_copy(side, place_here):
        return copy_to(
            parts.at[1 + side, place_here],
            returned.at[side, place_here],
            part_send.at[side, place_here],
            part_recv.at[side, place_here],
            from_sides[side],
        )

    def send_parts(i, carry):
        for side in range(3):
            part_copy(side, lax.rem(i, SPLIT)).start()
        return carry

    lax.fori_loop(1, SPLIT + 1, send_parts, 0)

    def column(i):
        return lax.rem(x + i, SPLIT)

    def sibling_copy(i):
        some = pl.ds(column(i) * SPLIT, SPLIT)
        return copy_to(
            grads.at[1 - core, some],
            sibling_grads.at[some],
            sibling_send.at[i],
            sibling_recv.at[i],
            sibling,
        )

    def weight_grads(i):
        c = column(i)
        cols = pl.ds(pl.multiple_of(c * STEP, STEP), STEP)
        left = rows_in[:, :, :, cols].reshape(n_rows, STEP)
        one = lax.dot_general(left, pair[...], FIRST, preferred_element_type=jnp.float32)
        left = rows_grad[:, :, :, cols].reshape(n_rows, STEP)
        two = lax.dot_general(left, active[...], FIRST, preferred_element_type=jnp.float32)
        one = one.astype(jnp.bfloat16).reshape(blocks, depth, 2 * hidden)
        two = two.reshape(blocks, 2, depth // 2, hidden)
        for b in range(blocks):
            to = c * (blocks // 2) + b // 2
            grads[b % 2, to, :depth] = one[b]
            grads[b % 2, to, depth:] = beside(two[b, 0], two[b, 1])
        sibling_copy(i).start()

    def grad_copy(to, h):
        return copy_to(
            grads.at[core, to, rows_of(h)],
            grads_in.at[chip, rows_of(h)],
            grad_send.at[to, h],
            grad_recv.at[chip, h],
            (2 * to + core, z),
        )

    def send_grads(i):
        some = sibling_grads.at[pl.ds(column(i) * SPLIT, SPLIT)]
        copy_to(some, some, sibling_send.at[i], sibling_recv.at[i], sibling).wait_recv()
        for step in range(SPLIT):
            to = column(i) * SPLIT + lax.rem(y + step, SPLIT)
            total = grads[core, to].astype(jnp.float32) + sibling_grads[to].astype(jnp.float32)
            grads[core, to] = total.astype(jnp.bfloat16)
            pl.when(to != chip)(grad_copy(to, 0).start)

    def grads_out(i, carry):
        weight_grads(i)

        @pl.when(i > 0)
        def _():
            send_grads(i - 1)

        return carry

    def send_later(to, carry):
        @pl.when(to != chip)
        def _():
            for h in range(1, PIECES):
                grad_copy(to, h).start()

        return carry

    lax.fori_loop(0, SPLIT, grads_out, 0)
    send_grads(SPLIT - 1)
    grads_in[chip] = grads[core, chip]
    lax.fori_loop(0, CHIPS, send_later, 0)

    def sum_parts(place_here):
        for side in range(3):
            copy_to(
                returned.at[side, place_here],
                returned.at[side, place_here],
                part_send.at[side, place_here],
                part_recv.at[side, place_here],
                sibling,
            ).wait_recv()
        total = parts[0, place_here].astype(jnp.float32)
        for side in range(3):
            total += returned[side, place_here].astype(jnp.float32)
        sums[place_here] = total.astype(jnp.bfloat16)

    def final_copy(place_here):
        late = place_here // 2
        distance = edge * ((1 - late) * 4 + late * (8 - place_here)) + (1 - edge) * (5 - place_here)
        to = edge * late + (1 - edge * late) * 2 * upper
        return copy_to(
            sums.at[place_here],
            finals.at[to],
            final_send.at[place_here],
            final_recv.at[to],
            plane((2 * upper - 1) * distance),
        )

    def send_finals(place_here, carry):
        sum_parts(place_here)
        final_copy(place_here).start()
        return carry

    lax.fori_loop(1, SPLIT, send_finals, 0)

    for copy in entries:
        copy.wait_send()

    def drain_in(i, carry):
        for h in range(PIECES):
            for to_y in range(SPLIT):
                elsewhere, copy = spread_copy(i, to_y, h)
                pl.when(elsewhere)(copy.wait_send)
        for side in range(3):
            for h in range(2):
                side_copy(side, i, h).wait_send()
        return carry

    lax.fori_loop(0, SPLIT, drain_in, 0)

    def drain_twins(i, carry):
        for h in range(PIECES):
            twin_copy(i, h).wait_send()
        return carry

    lax.fori_loop(0, CHIPS, drain_twins, 0)
    for h in range(PIECES):
        for i in range(1, SPLIT):
            shard_copy(i, h).wait_send()

    sum_parts(0)

    def finals_arrived(i, carry):
        copy_to(
            finals.at[i], finals.at[i], final_send.at[1], final_recv.at[i], sibling
        ).wait_recv()
        return carry

    lax.fori_loop(0, 3, finals_arrived, 0)
    where_from = jnp.concatenate(
        [
            place[lax.rem(group + 1, SPLIT)],
            place[lax.rem(group + 2, SPLIT)],
            place[lax.rem(group + 3, SPLIT)],
            place[group],
        ],
        axis=0,
    )

    def give_back(c, carry):
        cols = pl.ds(pl.multiple_of(c * STEP, STEP), STEP)
        values = jnp.concatenate(
            [finals[:, :, cols].reshape(3 * CAP, STEP), sums[0, :, cols]], axis=0
        )
        grad_tokens[:, cols] = lax.dot_general(
            where_from, values, FIRST, preferred_element_type=jnp.float32
        ).astype(jnp.bfloat16)
        return carry

    lax.fori_loop(0, chunks, give_back, 0)

    def plane_sum(part, h):
        total = jnp.zeros((piece, 2 * hidden), jnp.float32)
        for from_y in range(SPLIT):
            source = lax.rem(part + 2 * from_y, SPLIT) * SPLIT + from_y

            @pl.when(source != chip)
            def _():
                some = grads_in.at[source, rows_of(h)]
                copy_to(some, some, grad_send.at[0, h], grad_recv.at[source, h], sibling).wait_recv()

            total += grads_in[source, rows_of(h)].astype(jnp.float32)
        return total

    def group_copy(i, h):
        part = lax.rem(member + i, SPLIT)
        return copy_to(
            group_sums.at[i, rows_of(h)],
            group_in.at[SPLIT - i, rows_of(h)],
            group_send.at[i, h],
            group_recv.at[SPLIT - i, h],
            (dp, group * SPLIT + part),
        )

    def send_group(n, carry):
        h, i = n // 3, 1 + lax.rem(n, 3)
        group_sums[i, rows_of(h)] = plane_sum(lax.rem(member + i, SPLIT), h).astype(jnp.bfloat16)
        group_copy(i, h).start()
        return carry

    lax.fori_loop(0, 3 * PIECES, send_group, 0)

    def drain_out(i, carry):
        for side in range(3):
            part_copy(side, i).wait_send()
        sibling_copy(i).wait_send()
        return carry

    def drain_grads(i, carry):
        for h in range(PIECES):
            grad_copy(lax.rem(chip + i, CHIPS), h).wait_send()
        return carry

    lax.fori_loop(0, SPLIT, drain_out, 0)
    for i in range(1, SPLIT):
        final_copy(i).wait_send()
    lax.fori_loop(1, CHIPS, drain_grads, 0)

    total = jnp.concatenate([plane_sum(member, h) for h in range(PIECES)], axis=0)
    for i in range(1, SPLIT):
        for h in range(PIECES):
            some = group_in.at[i, rows_of(h)]
            copy_to(some, some, group_send.at[i, h], group_recv.at[i, h], sibling).wait_recv()
        total += group_in[i].astype(jnp.float32)
    grad_gate[...] = total[:depth, :hidden]
    grad_up[...] = total[:depth, hidden:]
    grad_down[: depth // 2] = total[depth:, :hidden]
    grad_down[depth // 2 :] = total[depth:, hidden:]

    for h in range(PIECES):
        for i in range(1, SPLIT):
            group_copy(i, h).wait_send()


def hand_over(*refs):
    sources, targets, held = refs[:4], refs[4:8], refs[8:12]
    reads = [pltpu.make_async_copy(sources[i], held[i], refs[12].at[i]) for i in range(4)]
    writes = [pltpu.make_async_copy(held[i], targets[i], refs[13].at[i]) for i in range(4)]
    for copy in reads:
        copy.start()
    for read, write in zip(reads, writes):
        read.wait()
        write.start()
    for copy in writes:
        copy.wait()


def body(tokens, cotangent, ids, mask, gates, gate_w, up_w, down_w):
    n_tok, width = tokens.shape
    top = ids.shape[1]
    depth, hidden = gate_w.shape
    tall = depth * 3 // 2
    n_rows = RING * CAP
    bf16, f32, i32 = jnp.bfloat16, jnp.float32, jnp.int32
    vmem = pl.BlockSpec(memory_space=pltpu.VMEM)
    dma = pltpu.SemaphoreType.DMA
    grad_tokens, grad_gate, grad_up, grad_down = pl.pallas_call(
        kernel,
        out_shape=(
            jax.ShapeDtypeStruct((n_tok, width), bf16),
            jax.ShapeDtypeStruct((depth, hidden), f32),
            jax.ShapeDtypeStruct((depth, hidden), f32),
            jax.ShapeDtypeStruct((depth, hidden), f32),
        ),
        in_specs=[pl.BlockSpec(memory_space=pltpu.HBM)] * 8,
        out_specs=[vmem] * 4,
        scratch_shapes=[
            pltpu.VMEM((n_tok, width), bf16),
            pltpu.VMEM((n_tok, width), bf16),
            pltpu.VMEM((top, n_tok), i32),
            pltpu.VMEM((top, n_tok), i32),
            pltpu.VMEM((top, n_tok), f32),
            pltpu.VMEM((depth, hidden), bf16),
            pltpu.VMEM((depth, hidden), bf16),
            pltpu.VMEM((depth, hidden), bf16),
            pltpu.VMEM((SPLIT, CAP, n_tok), bf16),
            pltpu.VMEM((SPLIT, SPLIT, CAP, width), bf16),
            pltpu.VMEM((SPLIT, SPLIT, CAP, width), bf16),
            pltpu.VMEM((SPLIT, CAP, width), bf16),
            pltpu.VMEM((SPLIT, CAP, width), bf16),
            pltpu.VMEM((SPLIT, tall, 2 * hidden), bf16),
            pltpu.VMEM((2 * CHIPS, tall, 2 * hidden), bf16),
            pltpu.VMEM((n_rows, 2 * hidden), f32),
            pltpu.VMEM((n_rows, hidden), f32),
            pltpu.VMEM((n_rows, 2 * hidden), bf16),
            pltpu.VMEM((n_rows, hidden), bf16),
            pltpu.VMEM((SPLIT, SPLIT, CAP, width), bf16),
            pltpu.VMEM((3, SPLIT, CAP, width), bf16),
            pltpu.VMEM((SPLIT, CAP, width), bf16),
            pltpu.VMEM((3, CAP, width), bf16),
            pltpu.VMEM((2, CHIPS, tall, 2 * hidden), bf16),
            pltpu.VMEM((CHIPS, tall, 2 * hidden), bf16),
            pltpu.VMEM((CHIPS, tall, 2 * hidden), bf16),
            pltpu.VMEM((SPLIT, tall, 2 * hidden), bf16),
            pltpu.VMEM((SPLIT, tall, 2 * hidden), bf16),
            dma((8,)),
            dma((3, 2)),
            dma((SPLIT, 2)),
            dma((3, SPLIT, 2)),
            dma((3, SPLIT, 2)),
            dma((SPLIT, PIECES)),
            dma((SPLIT, PIECES)),
            dma((SPLIT, SPLIT, PIECES)),
            dma((CHIPS, PIECES)),
            dma((CHIPS, PIECES)),
            dma((CHIPS, PIECES)),
            dma((3, SPLIT)),
            dma((3, SPLIT)),
            dma((SPLIT,)),
            dma((3,)),
            dma((SPLIT,)),
            dma((SPLIT,)),
            dma((CHIPS, PIECES)),
            dma((CHIPS, PIECES)),
            dma((SPLIT, PIECES)),
            dma((SPLIT, PIECES)),
        ],
        compiler_params=pltpu.CompilerParams(
            collective_id=0, has_side_effects=True, vmem_limit_bytes=VMEM_BYTES
        ),
        cost_estimate=pl.CostEstimate(
            flops=16 * n_rows * width * hidden, bytes_accessed=1 << 21, transcendentals=1 << 16
        ),
    )(tokens, cotangent, ids.T, mask.T, gates.T, gate_w, up_w, down_w.T)
    anywhere = pl.BlockSpec(memory_space=pl.ANY)
    results = (grad_tokens, grad_gate, grad_up, grad_down)
    grad_tokens, grad_gate, grad_up, grad_down = pl.pallas_call(
        hand_over,
        out_shape=tuple(jax.ShapeDtypeStruct(r.shape, r.dtype) for r in results),
        in_specs=[anywhere] * 4,
        out_specs=[anywhere] * 4,
        scratch_shapes=[pltpu.VMEM(r.shape, r.dtype) for r in results] + [dma((4,)), dma((4,))],
        compiler_params=pltpu.CompilerParams(vmem_limit_bytes=VMEM_BYTES),
    )(*results)
    return grad_tokens, grad_gate, grad_up, grad_down.T


def solution(mesh):
    rows = P(("dp", "expert"), None)
    return jax.shard_map(
        body,
        mesh=mesh,
        in_specs=(rows, rows, rows, rows, rows) + (P("dp", "expert"),) * 2 + (P("expert", "dp"),),
        out_specs=(rows, P("dp", "expert"), P("dp", "expert"), P("expert", "dp")),
        check_vma=False,
    )
```

```python
import functools

import jax
import jax.numpy as jnp
from jax import lax
from jax.experimental import pallas as pl
from jax.experimental.pallas import tpu as pltpu
from jax.sharding import PartitionSpec as P

MESH = pl.DeviceIdType.MESH
RING = 16
SPLIT = 4
CHIPS = SPLIT * SPLIT
CAP = 16
STEP = 512
VMEM_BYTES = 64 * 1024 * 1024 - 131072
PIECES = 2
LAST = (((1,), (1,)), ((), ()))
FIRST = (((0,), (0,)), ((), ()))


def copy_to(src, dst, send_sem, recv_sem, device):
    return pltpu.make_async_remote_copy(
        src_ref=src,
        dst_ref=dst,
        send_sem=send_sem,
        recv_sem=recv_sem,
        device_id=device,
        device_id_type=MESH,
    )


def beside(left, right):
    both = [left.astype(jnp.float32), right.astype(jnp.float32)]
    return jnp.concatenate(both, axis=-1).astype(jnp.bfloat16)


def kernel(
    tokens_hbm,
    cotangent_hbm,
    ids_hbm,
    mask_hbm,
    gates_hbm,
    gate_hbm,
    up_hbm,
    down_hbm,
    grad_tokens,
    grad_gate,
    grad_up,
    grad_down,
    tokens,
    cotangent,
    ids,
    mask,
    gates,
    gate_w,
    up_w,
    down_w,
    place,
    rows_in,
    rows_grad,
    out_in,
    out_grad,
    shards,
    weights,
    pre,
    act,
    pair,
    active,
    parts,
    returned,
    sums,
    finals,
    grads,
    sibling_grads,
    grads_in,
    group_sums,
    group_in,
    load_sem,
    entry_send,
    entry_recv,
    side_send,
    side_recv,
    shard_send,
    shard_recv,
    spread_send,
    spread_recv,
    twin_send,
    twin_recv,
    part_send,
    part_recv,
    final_send,
    final_recv,
    sibling_send,
    sibling_recv,
    grad_send,
    grad_recv,
    group_send,
    group_recv,
):
    width = tokens.shape[1]
    depth, hidden = gate_w.shape
    tall = weights.shape[1]
    piece = tall // PIECES
    n_tok = tokens.shape[0]
    n_rows = RING * CAP
    blocks = STEP // depth
    chunks = width // STEP

    dp = lax.axis_index("dp")
    z = lax.axis_index("expert")
    group = z // SPLIT
    member = lax.rem(z, SPLIT)
    core = lax.rem(dp, 2)
    chip = dp // 2
    x = chip // SPLIT
    y = lax.rem(chip, SPLIT)
    sibling = (dp + 1 - 2 * core, z)

    def plane(offset):
        return (dp, lax.rem(z + offset + RING, RING))

    def at(to_x, to_y):
        return ((lax.rem(to_x + SPLIT, SPLIT) * SPLIT + lax.rem(to_y + SPLIT, SPLIT)) * 2 + core, z)

    up_down = 1 - 2 * core
    to_sides = (at(x + 1, y), at(x - 1, y), at(x, y + up_down))
    from_sides = (at(x - 1, y), at(x + 1, y), at(x, y - up_down))

    loads = [
        pltpu.make_async_copy(source, target, load_sem.at[i])
        for i, (source, target) in enumerate(
            (
                (ids_hbm, ids),
                (mask_hbm, mask),
                (gates_hbm, gates),
                (tokens_hbm, tokens),
                (cotangent_hbm, cotangent),
                (gate_hbm, gate_w),
                (up_hbm, up_w),
                (down_hbm, down_w),
            )
        )
    ]
    for load in loads:
        load.start()

    barrier = pltpu.get_barrier_semaphore()

    def greet_ring(i, carry):
        pl.semaphore_signal(barrier, inc=1, device_id=plane(i), device_id_type=MESH)
        return carry

    def greet_plane(i, carry):
        pl.semaphore_signal(
            barrier, inc=1, device_id=(lax.rem(dp + 2 * i, 2 * CHIPS), z), device_id_type=MESH
        )
        return carry

    lax.fori_loop(1, RING, greet_ring, 0, unroll=True)
    lax.fori_loop(1, CHIPS, greet_plane, 0, unroll=True)
    pl.semaphore_signal(barrier, inc=1, device_id=sibling, device_id_type=MESH)

    for load in loads[:3]:
        load.wait()
    live = mask[...] == 1
    hits, gate_rows = [], []
    for j in range(SPLIT):
        hit = jnp.where((ids[...] == j) & live, 1.0, 0.0)
        hits.append(jnp.sum(hit, axis=0, keepdims=True))
        gate_rows.append(jnp.sum(hit * gates[...], axis=0, keepdims=True))
    hit_rows = jnp.concatenate(hits + [jnp.zeros((CAP - SPLIT, n_tok), jnp.float32)], axis=0)
    earlier = (
        lax.broadcasted_iota(jnp.int32, (n_tok, n_tok), 0)
        < lax.broadcasted_iota(jnp.int32, (n_tok, n_tok), 1)
    )
    rank = jnp.dot(
        hit_rows.astype(jnp.bfloat16),
        jnp.where(earlier, 1.0, 0.0).astype(jnp.bfloat16),
        preferred_element_type=jnp.float32,
    )
    slot = lax.broadcasted_iota(jnp.int32, (CAP, n_tok), 0).astype(jnp.float32)
    slot_gates = []
    for j in range(SPLIT):
        held = jnp.where(
            (jnp.broadcast_to(rank[j : j + 1], (CAP, n_tok)) == slot)
            & (jnp.broadcast_to(hits[j], (CAP, n_tok)) > 0.5),
            1.0,
            0.0,
        )
        place[j] = held.astype(jnp.bfloat16)
        slot_gates.append(jnp.sum(held * gate_rows[j], axis=1, keepdims=True))
    slot_gate = jnp.concatenate(slot_gates, axis=0)
    chosen = place[...].reshape(SPLIT * CAP, n_tok)

    for load in loads[3:]:
        load.wait()

    def fill(c, carry):
        cols = pl.ds(pl.multiple_of(c * STEP, STEP), STEP)
        picked = jnp.dot(chosen, tokens[:, cols], preferred_element_type=jnp.float32)
        out_in[:, :, cols] = picked.astype(jnp.bfloat16).reshape(SPLIT, CAP, STEP)
        picked = jnp.dot(chosen, cotangent[:, cols], preferred_element_type=jnp.float32)
        out_grad[:, :, cols] = (
            (slot_gate * picked).astype(jnp.bfloat16).reshape(SPLIT, CAP, STEP)
        )
        return carry

    lax.fori_loop(0, chunks, fill, 0, unroll=True)
    rows_in[0, 0] = out_in[group]
    rows_grad[0, 0] = out_grad[group]

    shards[member, :depth] = beside(gate_w[...], up_w[...])
    shards[member, depth:] = beside(down_w[: depth // 2], down_w[depth // 2 :])

    pl.semaphore_wait(barrier, RING - 1 + CHIPS)

    both = ((out_in, rows_in), (out_grad, rows_grad))
    upper = member // 2
    edge = 1 - lax.rem((member + 1) // 2, 2)
    low = (1 - upper) * edge
    high = upper * edge
    entries = []
    for index, offset, place_there, expert in (
        (
            1,
            upper * (8 - member) - (1 - upper) * (member + 5),
            upper * member + (1 - upper) * (3 - member),
            lax.rem(group + 2, SPLIT),
        ),
        (0, 5 - member - low, member + low, lax.rem(group + 1, SPLIT)),
        (2, high - member - 2, 3 - member + high, lax.rem(group + 3, SPLIT)),
    ):
        for h, (source, rows) in enumerate(both):
            entries.append(
                copy_to(
                    source.at[expert],
                    rows.at[0, place_there],
                    entry_send.at[index, h],
                    entry_recv.at[place_there, h],
                    plane(offset),
                )
            )

    def rows_of(h):
        return pl.ds(h * piece, piece)

    def shard_copy(i, h):
        return copy_to(
            shards.at[member, rows_of(h)],
            shards.at[member, rows_of(h)],
            shard_send.at[i, h],
            shard_recv.at[member, h],
            (dp, group * SPLIT + lax.rem(member + i, SPLIT)),
        )

    def spread_copy(part, to_y, h):
        to_x = lax.rem(part + 2 * to_y, SPLIT)
        return (
            (to_x * SPLIT + to_y) != chip,
            copy_to(
                shards.at[part, rows_of(h)],
                weights.at[dp, rows_of(h)],
                spread_send.at[part, to_y, h],
                spread_recv.at[chip, h],
                at(to_x, to_y),
            ),
        )

    def spread(h, i):
        part = lax.rem(member + i, SPLIT)

        @pl.when(i > 0)
        def _():
            some = shards.at[part, rows_of(h)]
            copy_to(
                some, some, shard_send.at[0, h], shard_recv.at[part, h], sibling
            ).wait_recv()

        for step in range(SPLIT):
            to_y = lax.rem(y + step, SPLIT)
            elsewhere, copy = spread_copy(part, to_y, h)
            pl.when(elsewhere)(copy.start)

    def spread_rest(n, carry):
        spread(n // 3, 1 + lax.rem(n, 3))
        return carry

    def spread_own(h, carry):
        spread(h, 0)
        return carry

    for h in range(PIECES):
        for i in range(1, SPLIT):
            shard_copy(i, h).start()
    for copy in entries:
        copy.start()


    def side_copy(side, place_here, h):
        rows = both[h][1]
        return copy_to(
            rows.at[0, place_here],
            rows.at[1 + side, place_here],
            side_send.at[side, place_here, h],
            side_recv.at[side, place_here, h],
            to_sides[side],
        )

    def send_sides(place_here):
        for h in range(2):
            for side in range(3):
                side_copy(side, place_here, h).start()

    send_sides(0)
    lax.fori_loop(0, PIECES, spread_own, 0)
    lax.fori_loop(0, 3 * PIECES, spread_rest, 0)

    my_part = lax.rem(x + 2 * y, SPLIT)
    weights[dp] = shards[my_part]

    def twin_copy(i, h):
        some = weights.at[lax.rem(chip + i, CHIPS) * 2 + core, rows_of(h)]
        return copy_to(some, some, twin_send.at[i, h], twin_recv.at[i, h], sibling)

    for h in range(PIECES):
        twin_copy(0, h).start()

    def twin(h):
        def one(i, carry):
            source = lax.rem(chip + i, CHIPS)
            some = weights.at[source * 2 + core, rows_of(h)]
            copy_to(
                some, some, twin_send.at[i, h], spread_recv.at[source, h], sibling
            ).wait_recv()
            twin_copy(i, h).start()
            return carry

        lax.fori_loop(1, CHIPS, one, 0)

    def pass_sides(place_here, carry):
        for h, (_, rows) in enumerate(both):
            copy_to(
                rows.at[0, place_here],
                rows.at[0, place_here],
                entry_send.at[0, h],
                entry_recv.at[place_here, h],
                sibling,
            ).wait_recv()
            for side in range(3):
                side_copy(side, place_here, h).start()
        return carry

    pass_sides(1, 0)
    twin(0)
    pass_sides(2, 0)
    pass_sides(3, 0)
    twin(1)

    def sides_arrived(place_here, carry):
        for side in range(3):
            for h, (_, rows) in enumerate(both):
                copy_to(
                    rows.at[1 + side, place_here],
                    rows.at[1 + side, place_here],
                    side_send.at[side, place_here, h],
                    side_recv.at[side, place_here, h],
                    sibling,
                ).wait_recv()
        return carry

    lax.fori_loop(0, SPLIT, sides_arrived, 0)

    def twins_arrived(i, carry):
        for h in range(PIECES):
            some = weights.at[lax.rem(chip + i, CHIPS) * 2 + 1 - core, rows_of(h)]
            copy_to(some, some, twin_send.at[i, h], twin_recv.at[i, h], sibling).wait_recv()
        return carry

    lax.fori_loop(0, CHIPS, twins_arrived, 0)

    pre[...] = jnp.zeros_like(pre)
    act[...] = jnp.zeros_like(act)

    def project(c, carry):
        cols = pl.ds(pl.multiple_of(c * STEP, STEP), STEP)
        some = pl.ds(c * blocks, blocks)
        block = weights[some, :depth].reshape(STEP, 2 * hidden)
        left = rows_in[:, :, :, cols].reshape(n_rows, STEP)
        pre[...] += jnp.dot(left, block, preferred_element_type=jnp.float32)
        below = weights[some, depth:]
        block = jnp.concatenate([below[:, :, :hidden], below[:, :, hidden:]], axis=1)
        left = rows_grad[:, :, :, cols].reshape(n_rows, STEP)
        act[...] += jnp.dot(
            left, block.reshape(STEP, hidden), preferred_element_type=jnp.float32
        )
        return carry

    lax.fori_loop(0, chunks, project, 0, unroll=True)

    pre_gate = pre[:, :hidden]
    pre_up = pre[:, hidden:]
    grad_act = act[...]
    sigmoid_value = jax.nn.sigmoid(pre_gate)
    silu_value = pre_gate * sigmoid_value
    slope = sigmoid_value * (1.0 + pre_gate * (1.0 - sigmoid_value))
    pair[...] = jnp.concatenate(
        [grad_act * pre_up * slope, grad_act * silu_value], axis=1
    ).astype(jnp.bfloat16)
    active[...] = (silu_value * pre_up).astype(jnp.bfloat16)

    def back_project(c, carry):
        cols = pl.ds(pl.multiple_of(c * STEP, STEP), STEP)
        block = weights[pl.ds(c * blocks, blocks), :depth].reshape(STEP, 2 * hidden)
        part = lax.dot_general(pair[...], block, LAST, preferred_element_type=jnp.float32)
        parts[:, :, :, cols] = part.astype(jnp.bfloat16).reshape(SPLIT, SPLIT, CAP, STEP)
        return carry

    lax.fori_loop(0, chunks, back_project, 0, unroll=True)

    def part_copy(side, place_here):
        return copy_to(
            parts.at[1 + side, place_here],
            returned.at[side, place_here],
            part_send.at[side, place_here],
            part_recv.at[side, place_here],
            from_sides[side],
        )

    def far_first(i):
        return (1 - edge) * i + edge * (1 + lax.rem(i, 3))

    def send_parts(i, carry):
        for side in range(3):
            part_copy(side, far_first(i)).start()
        return carry

    lax.fori_loop(1, SPLIT, send_parts, 0)
    for side in range(3):
        part_copy(side, 0).start()

    def column(i):
        return lax.rem(x + i, SPLIT)

    def sibling_copy(i):
        some = pl.ds(column(i) * SPLIT, SPLIT)
        return copy_to(
            grads.at[1 - core, some],
            sibling_grads.at[some],
            sibling_send.at[i],
            sibling_recv.at[i],
            sibling,
        )

    def weight_grads(i):
        c = column(i)
        cols = pl.ds(pl.multiple_of(c * STEP, STEP), STEP)
        left = rows_in[:, :, :, cols].reshape(n_rows, STEP)
        one = lax.dot_general(left, pair[...], FIRST, preferred_element_type=jnp.float32)
        left = rows_grad[:, :, :, cols].reshape(n_rows, STEP)
        two = lax.dot_general(left, active[...], FIRST, preferred_element_type=jnp.float32)
        one = one.astype(jnp.bfloat16).reshape(blocks, depth, 2 * hidden)
        two = two.reshape(blocks, 2, depth // 2, hidden)
        for b in range(blocks):
            to = c * (blocks // 2) + b // 2
            grads[b % 2, to, :depth] = one[b]
            grads[b % 2, to, depth:] = beside(two[b, 0], two[b, 1])
        sibling_copy(i).start()

    def grad_copy(to, h):
        return copy_to(
            grads.at[core, to, rows_of(h)],
            grads_in.at[chip, rows_of(h)],
            grad_send.at[to, h],
            grad_recv.at[chip, h],
            (2 * to + core, z),
        )

    def send_grads(i):
        some = sibling_grads.at[pl.ds(column(i) * SPLIT, SPLIT)]
        copy_to(some, some, sibling_send.at[i], sibling_recv.at[i], sibling).wait_recv()
        for step in range(SPLIT):
            to = column(i) * SPLIT + lax.rem(y + step, SPLIT)
            total = grads[core, to].astype(jnp.float32) + sibling_grads[to].astype(jnp.float32)
            grads[core, to] = total.astype(jnp.bfloat16)
            pl.when(to != chip)(grad_copy(to, 0).start)

    def grads_out(i, carry):
        weight_grads(i)

        @pl.when(i > 0)
        def _():
            send_grads(i - 1)

        return carry

    def send_later(to, carry):
        @pl.when(to != chip)
        def _():
            for h in range(1, PIECES):
                grad_copy(to, h).start()

        return carry

    lax.fori_loop(0, SPLIT, grads_out, 0)
    send_grads(SPLIT - 1)
    grads_in[chip] = grads[core, chip]
    lax.fori_loop(0, CHIPS, send_later, 0)

    def sum_parts(place_here):
        for side in range(3):
            copy_to(
                returned.at[side, place_here],
                returned.at[side, place_here],
                part_send.at[side, place_here],
                part_recv.at[side, place_here],
                sibling,
            ).wait_recv()
        total = parts[0, place_here].astype(jnp.float32)
        for side in range(3):
            total += returned[side, place_here].astype(jnp.float32)
        sums[place_here] = total.astype(jnp.bfloat16)

    def final_copy(place_here):
        late = place_here // 2
        distance = edge * ((1 - late) * 4 + late * (8 - place_here)) + (1 - edge) * (5 - place_here)
        to = edge * late + (1 - edge * late) * 2 * upper
        return copy_to(
            sums.at[place_here],
            finals.at[to],
            final_send.at[place_here],
            final_recv.at[to],
            plane((2 * upper - 1) * distance),
        )

    def send_finals(i, carry):
        place_here = far_first(i)
        sum_parts(place_here)
        final_copy(place_here).start()
        return carry

    lax.fori_loop(1, SPLIT, send_finals, 0)

    for copy in entries:
        copy.wait_send()

    def drain_in(i, carry):
        for h in range(PIECES):
            for to_y in range(SPLIT):
                elsewhere, copy = spread_copy(i, to_y, h)
                pl.when(elsewhere)(copy.wait_send)
        for side in range(3):
            for h in range(2):
                side_copy(side, i, h).wait_send()
        return carry

    lax.fori_loop(0, SPLIT, drain_in, 0)

    def drain_twins(i, carry):
        for h in range(PIECES):
            twin_copy(i, h).wait_send()
        return carry

    lax.fori_loop(0, CHIPS, drain_twins, 0)
    for h in range(PIECES):
        for i in range(1, SPLIT):
            shard_copy(i, h).wait_send()

    sum_parts(0)

    def finals_arrived(i, carry):
        copy_to(
            finals.at[i], finals.at[i], final_send.at[1], final_recv.at[i], sibling
        ).wait_recv()
        return carry

    lax.fori_loop(0, 3, finals_arrived, 0)
    where_from = jnp.concatenate(
        [
            place[lax.rem(group + 1, SPLIT)],
            place[lax.rem(group + 2, SPLIT)],
            place[lax.rem(group + 3, SPLIT)],
            place[group],
        ],
        axis=0,
    )

    def give_back(c, carry):
        cols = pl.ds(pl.multiple_of(c * STEP, STEP), STEP)
        values = jnp.concatenate(
            [finals[:, :, cols].reshape(3 * CAP, STEP), sums[0, :, cols]], axis=0
        )
        grad_tokens[:, cols] = lax.dot_general(
            where_from, values, FIRST, preferred_element_type=jnp.float32
        ).astype(jnp.bfloat16)
        return carry

    lax.fori_loop(0, chunks, give_back, 0, unroll=True)

    def plane_sum(part, h):
        total = jnp.zeros((piece, 2 * hidden), jnp.float32)
        for from_y in range(SPLIT):
            source = lax.rem(part + 2 * from_y, SPLIT) * SPLIT + from_y

            @pl.when(source != chip)
            def _():
                some = grads_in.at[source, rows_of(h)]
                copy_to(some, some, grad_send.at[0, h], grad_recv.at[source, h], sibling).wait_recv()

            total += grads_in[source, rows_of(h)].astype(jnp.float32)
        return total

    def group_copy(i, h):
        part = lax.rem(member + i, SPLIT)
        return copy_to(
            group_sums.at[i, rows_of(h)],
            group_in.at[SPLIT - i, rows_of(h)],
            group_send.at[i, h],
            group_recv.at[SPLIT - i, h],
            (dp, group * SPLIT + part),
        )

    def send_group(n, carry):
        h, i = n // 3, 1 + lax.rem(n, 3)
        group_sums[i, rows_of(h)] = plane_sum(lax.rem(member + i, SPLIT), h).astype(jnp.bfloat16)
        group_copy(i, h).start()
        return carry

    lax.fori_loop(0, 3 * PIECES, send_group, 0)

    def drain_out(i, carry):
        for side in range(3):
            part_copy(side, i).wait_send()
        sibling_copy(i).wait_send()
        return carry

    def drain_grads(i, carry):
        for h in range(PIECES):
            grad_copy(lax.rem(chip + i, CHIPS), h).wait_send()
        return carry

    lax.fori_loop(0, SPLIT, drain_out, 0)
    for i in range(1, SPLIT):
        final_copy(i).wait_send()
    lax.fori_loop(1, CHIPS, drain_grads, 0)

    total = jnp.concatenate([plane_sum(member, h) for h in range(PIECES)], axis=0)
    for i in range(1, SPLIT):
        for h in range(PIECES):
            some = group_in.at[i, rows_of(h)]
            copy_to(some, some, group_send.at[i, h], group_recv.at[i, h], sibling).wait_recv()
        total += group_in[i].astype(jnp.float32)
    grad_gate[...] = total[:depth, :hidden]
    grad_up[...] = total[:depth, hidden:]
    grad_down[: depth // 2] = total[depth:, :hidden]
    grad_down[depth // 2 :] = total[depth:, hidden:]

    for h in range(PIECES):
        for i in range(1, SPLIT):
            group_copy(i, h).wait_send()


def hand_over(*refs):
    sources, targets, held = refs[:4], refs[4:8], refs[8:12]
    reads = [pltpu.make_async_copy(sources[i], held[i], refs[12].at[i]) for i in range(4)]
    writes = [pltpu.make_async_copy(held[i], targets[i], refs[13].at[i]) for i in range(4)]
    for copy in reads:
        copy.start()
    for read, write in zip(reads, writes):
        read.wait()
        write.start()
    for copy in writes:
        copy.wait()


def body(tokens, cotangent, ids, mask, gates, gate_w, up_w, down_w):
    n_tok, width = tokens.shape
    top = ids.shape[1]
    depth, hidden = gate_w.shape
    tall = depth * 3 // 2
    n_rows = RING * CAP
    bf16, f32, i32 = jnp.bfloat16, jnp.float32, jnp.int32
    vmem = pl.BlockSpec(memory_space=pltpu.VMEM)
    dma = pltpu.SemaphoreType.DMA
    grad_tokens, grad_gate, grad_up, grad_down = pl.pallas_call(
        kernel,
        out_shape=(
            jax.ShapeDtypeStruct((n_tok, width), bf16),
            jax.ShapeDtypeStruct((depth, hidden), f32),
            jax.ShapeDtypeStruct((depth, hidden), f32),
            jax.ShapeDtypeStruct((depth, hidden), f32),
        ),
        in_specs=[pl.BlockSpec(memory_space=pltpu.HBM)] * 8,
        out_specs=[vmem] * 4,
        scratch_shapes=[
            pltpu.VMEM((n_tok, width), bf16),
            pltpu.VMEM((n_tok, width), bf16),
            pltpu.VMEM((top, n_tok), i32),
            pltpu.VMEM((top, n_tok), i32),
            pltpu.VMEM((top, n_tok), f32),
            pltpu.VMEM((depth, hidden), bf16),
            pltpu.VMEM((depth, hidden), bf16),
            pltpu.VMEM((depth, hidden), bf16),
            pltpu.VMEM((SPLIT, CAP, n_tok), bf16),
            pltpu.VMEM((SPLIT, SPLIT, CAP, width), bf16),
            pltpu.VMEM((SPLIT, SPLIT, CAP, width), bf16),
            pltpu.VMEM((SPLIT, CAP, width), bf16),
            pltpu.VMEM((SPLIT, CAP, width), bf16),
            pltpu.VMEM((SPLIT, tall, 2 * hidden), bf16),
            pltpu.VMEM((2 * CHIPS, tall, 2 * hidden), bf16),
            pltpu.VMEM((n_rows, 2 * hidden), f32),
            pltpu.VMEM((n_rows, hidden), f32),
            pltpu.VMEM((n_rows, 2 * hidden), bf16),
            pltpu.VMEM((n_rows, hidden), bf16),
            pltpu.VMEM((SPLIT, SPLIT, CAP, width), bf16),
            pltpu.VMEM((3, SPLIT, CAP, width), bf16),
            pltpu.VMEM((SPLIT, CAP, width), bf16),
            pltpu.VMEM((3, CAP, width), bf16),
            pltpu.VMEM((2, CHIPS, tall, 2 * hidden), bf16),
            pltpu.VMEM((CHIPS, tall, 2 * hidden), bf16),
            pltpu.VMEM((CHIPS, tall, 2 * hidden), bf16),
            pltpu.VMEM((SPLIT, tall, 2 * hidden), bf16),
            pltpu.VMEM((SPLIT, tall, 2 * hidden), bf16),
            dma((8,)),
            dma((3, 2)),
            dma((SPLIT, 2)),
            dma((3, SPLIT, 2)),
            dma((3, SPLIT, 2)),
            dma((SPLIT, PIECES)),
            dma((SPLIT, PIECES)),
            dma((SPLIT, SPLIT, PIECES)),
            dma((CHIPS, PIECES)),
            dma((CHIPS, PIECES)),
            dma((CHIPS, PIECES)),
            dma((3, SPLIT)),
            dma((3, SPLIT)),
            dma((SPLIT,)),
            dma((3,)),
            dma((SPLIT,)),
            dma((SPLIT,)),
            dma((CHIPS, PIECES)),
            dma((CHIPS, PIECES)),
            dma((SPLIT, PIECES)),
            dma((SPLIT, PIECES)),
        ],
        compiler_params=pltpu.CompilerParams(
            collective_id=0, has_side_effects=True, vmem_limit_bytes=VMEM_BYTES
        ),
        cost_estimate=pl.CostEstimate(
            flops=16 * n_rows * width * hidden, bytes_accessed=1 << 21, transcendentals=1 << 16
        ),
    )(tokens, cotangent, ids.T, mask.T, gates.T, gate_w, up_w, down_w.T)
    anywhere = pl.BlockSpec(memory_space=pl.ANY)
    results = (grad_tokens, grad_gate, grad_up, grad_down)
    grad_tokens, grad_gate, grad_up, grad_down = pl.pallas_call(
        hand_over,
        out_shape=tuple(jax.ShapeDtypeStruct(r.shape, r.dtype) for r in results),
        in_specs=[anywhere] * 4,
        out_specs=[anywhere] * 4,
        scratch_shapes=[pltpu.VMEM(r.shape, r.dtype) for r in results] + [dma((4,)), dma((4,))],
        compiler_params=pltpu.CompilerParams(vmem_limit_bytes=VMEM_BYTES),
    )(*results)
    return grad_tokens, grad_gate, grad_up, grad_down.T


def solution(mesh):
    rows = P(("dp", "expert"), None)
    return jax.shard_map(
        body,
        mesh=mesh,
        in_specs=(rows, rows, rows, rows, rows) + (P("dp", "expert"),) * 2 + (P("expert", "dp"),),
        out_specs=(rows, P("dp", "expert"), P("dp", "expert"), P("expert", "dp")),
        check_vma=False,
    )
```
